512 devices in a mesh: gx: 8 (over y_hi, core), yz: 64 (over z, x, y_lo).
Axes of the slice: x: 4, y: 8 (y_hi: 4, y_lo: 2; y = y_hi * 2 + y_lo), z: 8, core: 2. Of those that a mesh axis runs over, the one named last changes fastest.
Arguments:
- snapshot: float32 [1024, 65536], P('gx', 'yz'), may hold values from -40 to 40, as said below
- start: float32 [1024, 192], replicated, may hold values from -6 to 6
Outputs:
- basis: float32 [1024, 192], P('gx')
- projected: float32 [1024, 65536], P('gx', 'yz')
The draws below stay inside these ranges and needn't reach their ends.
Inputs may be any that keep to these rules, and one draw needn't show every extreme that they name: Each x row of the snapshot has its own scale between 1 and 10; entries are independent.
All inputs are finite; a program needn't handle non-finite values.
Results may differ from the reference program's by a relative error of at most 0.00022.
Values sent between devices are 32-bit elements; how exact they have to be, the bound alone decides.
A program may use at most 64 MiB of HBM per device.

```python
import math
import jax
import jax.numpy as jnp
from jax import lax

NX = 1024
RANK = 192
ITERS = 4
CELLS = 65536


def draw_snapshot(key, part):
    key = jax.random.fold_in(key, 11)
    scale_key, entry_key = jax.random.split(key)
    scales = jnp.exp(jax.random.uniform(scale_key, (NX, 1), jnp.float32) * math.log(10.0))
    entries = jnp.clip(jax.random.normal(entry_key, (NX, CELLS), jnp.float32), -4.0, 4.0)
    return (scales * entries).astype(jnp.float32)


def normal_values(key, dims, deviation, bound, dtype=jnp.bfloat16):
    array = jax.random.normal(key, dims, jnp.float32) * deviation
    return jnp.minimum(jnp.maximum(array, -bound), bound).astype(dtype)


def setup_inputs(seed: int = 0) -> dict:
    key_list = jax.random.split(jax.random.key(seed), 3)
    snapshot = draw_snapshot(jax.random.fold_in(key_list[2], 71), 0)
    start = normal_values(key_list[1], (NX, RANK), 1.0, 6.0, jnp.float32)
    return {"snapshot": snapshot, "start": start}


def reference(snapshot, start):
    gram = jnp.dot(snapshot, snapshot.T, precision=lax.Precision.HIGHEST) / CELLS
    basis = start
    for step in range(ITERS):
        image = jnp.dot(gram, basis, precision=lax.Precision.HIGHEST)
        inner = jnp.dot(image.T, image, precision=lax.Precision.HIGHEST)
        lower = jnp.linalg.cholesky(inner)
        basis = jax.scipy.linalg.solve_triangular(lower, image.T, lower=True).T
    core = jnp.dot(basis.T, snapshot, precision=lax.Precision.HIGHEST)
    projected = jnp.dot(basis, core, precision=lax.Precision.HIGHEST)
    return (basis, projected)
```

```python
import functools
import jax
import jax.numpy as jnp
from jax import lax
from jax.experimental import pallas as pl
from jax.experimental.pallas import tpu as pltpu
from jax.sharding import PartitionSpec as P

ITERS = 4
G, NYH, NZ, NX, NYL = 8, 4, 8, 4, 2
ROWS = 128
NB = 5
XROWS = NB * ROWS // NX
ZROWS = 24
PAD = NZ * ZROWS
N = 1024
RANK = 192
PANEL = 32
GROUP = 4
f32, bf16 = jnp.float32, jnp.bfloat16
MESH = pl.DeviceIdType.MESH


def split2(a):
    hi = a.astype(jnp.bfloat16)
    lo = (a - hi.astype(jnp.float32)).astype(jnp.bfloat16)
    return hi, lo


def dot_nt(a, b):
    return lax.dot_general(a, b, (((1,), (1,)), ((), ())), preferred_element_type=jnp.float32)


def gram_kernel(cells, s_ref, d_ref, f_ref, lhs, parts, xin, xsum, zin, zsum, yin, send, recv, local):
    g = lax.axis_index("gx")
    q = lax.axis_index("yz")
    yh, core = g // 2, g % 2
    z, x, yl = q // (NX * NYL), (q // NYL) % NX, q % NYL

    def gx_at(yh2, core2):
        return yh2 * 2 + core2

    def yz_at(z2, x2, yl2):
        return (z2 * NX + x2) * NYL + yl2

    pair = (gx_at(yh, 1 - core), q)
    up = [(gx_at((yh + k) % NYH, core), q) for k in range(NYH)]
    xs = [(g, yz_at(z, (x + k) % NX, yl)) for k in range(NX)]
    zs = [(g, yz_at((z + k) % NZ, x, yl)) for k in range(NZ)]
    ylo = (g, yz_at(z, x, 1 - yl))
    peers = [pair] + up[1:] + xs[1:] + zs[1:] + [ylo]

    barrier = pltpu.get_barrier_semaphore()
    for peer in peers:
        pl.semaphore_signal(barrier, inc=1, device_id=peer, device_id_type=MESH)
    pl.semaphore_wait(barrier, len(peers))

    sent = []
    count = [0]

    def slot():
        count[0] += 1
        return count[0] - 1

    def copy(src, dst, index, target):
        return pltpu.make_async_remote_copy(
            src_ref=src, dst_ref=dst, send_sem=send.at[index], recv_sem=recv.at[index],
            device_id=target, device_id_type=MESH)

    def push(src, dst, index, target):
        op = copy(src, dst, index, target)
        op.start()
        sent.append(op)

    def arrived(dst, index):
        copy(dst, dst, index, pair).wait_recv()

    half = ROWS // 2

    def chunk(block, c):
        return d_ref.at[block, pl.ds(c * half, half), :]

    s_own, s_right, s_left, s_opp = slot(), [slot(), slot()], [slot(), slot()], [slot(), slot()]
    s_pair = {(k, c): slot() for k in range(3) for c in range(2)}
    right, left = up[1], up[3]
    g_left, g_right, g_opp = left[0], right[0], up[2][0]
    for c in (0, 1):
        push(s_ref.at[pl.ds(c * half, half), :], chunk(g, c), s_right[c], right)
        push(s_ref.at[pl.ds((1 - c) * half, half), :], chunk(g, 1 - c), s_left[1 - c], left)
    push(s_ref, d_ref.at[g], s_own, pair)
    mine = pltpu.make_async_copy(s_ref, d_ref.at[g], local)
    mine.start()

    hi, lo = split2(s_ref[...])
    lhs[pl.ds(0, ROWS), :] = hi
    lhs[pl.ds(ROWS, ROWS), :] = lo
    mine.wait()

    arrived(chunk(g_left, 0), s_right[0])
    push(chunk(g_left, 0), chunk(g_left, 0), s_opp[0], right)
    push(chunk(g_left, 0), chunk(g_left, 0), s_pair[0, 0], pair)
    arrived(chunk(g_right, 1), s_left[1])
    push(chunk(g_right, 1), chunk(g_right, 1), s_opp[1], left)
    push(chunk(g_right, 1), chunk(g_right, 1), s_pair[1, 1], pair)
    arrived(chunk(g_left, 1), s_right[1])
    push(chunk(g_left, 1), chunk(g_left, 1), s_pair[0, 1], pair)
    arrived(chunk(g_right, 0), s_left[0])
    push(chunk(g_right, 0), chunk(g_right, 0), s_pair[1, 0], pair)
    arrived(chunk(g_opp, 0), s_opp[0])
    push(chunk(g_opp, 0), chunk(g_opp, 0), s_pair[2, 0], pair)
    arrived(chunk(g_opp, 1), s_opp[1])
    push(chunk(g_opp, 1), chunk(g_opp, 1), s_pair[2, 1], pair)
    other = pair[0]
    arrived(d_ref.at[other], s_own)
    for k, step in enumerate((3, 1, 2)):
        block = gx_at((yh + step) % NYH, 1 - core)
        for c in range(2):
            arrived(chunk(block, c), s_pair[k, c])

    for d in range(NB):
        b_hi, b_lo = split2(d_ref[(g + d) % G])
        both = dot_nt(lhs[...], b_hi)
        part = both[:ROWS] + both[ROWS:] + dot_nt(lhs[pl.ds(0, ROWS), :], b_lo)
        part = part * (1.0 / cells)
        for k in range(NX):
            parts[k, pl.ds(32 * d, 32), :] = part[32 * k:32 * k + 32]

    s_x = [slot() for _ in range(NX - 1)]
    for k in range(1, NX):
        push(parts.at[(x + k) % NX], xin.at[k - 1], s_x[k - 1], xs[k])
    xsum[pl.ds(XROWS, PAD - XROWS), :] = jnp.zeros((PAD - XROWS, 128), jnp.float32)
    total = parts[x]
    for k in range(1, NX):
        arrived(xin.at[k - 1], s_x[k - 1])
        total += xin[k - 1]
    xsum[pl.ds(0, XROWS), :] = total

    def z_rows(z2):
        return pl.ds(pl.multiple_of(z2 * ZROWS, 8), ZROWS)

    s_z = [slot() for _ in range(NZ - 1)]
    for k in range(1, NZ):
        push(xsum.at[z_rows((z + k) % NZ), :], zin.at[k - 1], s_z[k - 1], zs[k])
    total = xsum[z_rows(z), :]
    for k in range(1, NZ):
        arrived(zin.at[k - 1], s_z[k - 1])
        total += zin[k - 1]
    zsum[...] = total
    s_yl = slot()
    push(zsum, yin, s_yl, ylo)
    arrived(yin, s_yl)
    f_ref[core, x, yh, z_rows(z), :] = zsum[...] + yin[...]

    s_ay = [slot() for _ in range(NYH - 1)]
    for k in range(1, NYH):
        block = f_ref.at[core, x, yh, z_rows(z), :]
        push(block, block, s_ay[k - 1], up[k])
    for k in range(1, NYH):
        arrived(f_ref.at[core, x, (yh - k + NYH) % NYH, z_rows(z), :], s_ay[k - 1])
    s_az = [slot() for _ in range(NZ - 1)]
    for k in range(1, NZ):
        block = f_ref.at[core, x, :, z_rows(z), :]
        push(block, block, s_az[k - 1], zs[k])
    for k in range(1, NZ):
        arrived(f_ref.at[core, x, :, z_rows((z - k + NZ) % NZ), :], s_az[k - 1])

    def x_block(core2, x2):
        return f_ref.at[core2, x2, :, pl.ds(0, XROWS), :]

    s_ax = [slot() for _ in range(NX - 1)]
    s_ap = [slot() for _ in range(NX)]
    for k in range(1, NX):
        push(x_block(core, x), x_block(core, x), s_ax[k - 1], xs[k])
    push(x_block(core, x), x_block(core, x), s_ap[0], pair)
    for k in range(1, NX):
        x2 = (x - k + NX) % NX
        arrived(x_block(core, x2), s_ax[k - 1])
        push(x_block(core, x2), x_block(core, x2), s_ap[k], pair)
    for k in range(NX):
        arrived(x_block(1 - core, (x - k + NX) % NX), s_ap[k])
    for op in sent:
        op.wait_send()


SLOTS = 13 + 3 + 7 + 1 + 3 + 7 + 3 + 4


def gather_and_gram(snapshot, all_cells):

    cols = snapshot.shape[1]
    f32 = jnp.float32
    return pl.pallas_call(
        functools.partial(gram_kernel, all_cells),
        out_shape=(jax.ShapeDtypeStruct((G, ROWS, cols), f32),
                   jax.ShapeDtypeStruct((2, NX, NYH, PAD, 128), f32)),
        in_specs=[pl.BlockSpec(memory_space=pltpu.VMEM)],
        out_specs=(pl.BlockSpec(memory_space=pltpu.VMEM), pl.BlockSpec(memory_space=pltpu.VMEM)),
        scratch_shapes=[
            pltpu.VMEM((2 * ROWS, cols), jnp.bfloat16),
            pltpu.VMEM((NX, XROWS, 128), f32),
            pltpu.VMEM((NX - 1, XROWS, 128), f32),
            pltpu.VMEM((PAD, 128), f32),
            pltpu.VMEM((NZ - 1, ZROWS, 128), f32),
            pltpu.VMEM((ZROWS, 128), f32),
            pltpu.VMEM((ZROWS, 128), f32),
            pltpu.SemaphoreType.DMA((SLOTS,)),
            pltpu.SemaphoreType.DMA((SLOTS,)),
            pltpu.SemaphoreType.DMA,
        ],
        compiler_params=pltpu.CompilerParams(
            collective_id=0, has_side_effects=True, vmem_limit_bytes=40 * 2**20),
    )(snapshot)


def dot(a, b):
    return lax.dot_general(a, b, (((1,), (0,)), ((), ())), preferred_element_type=f32)


def dot3(a, b_hi, b_lo, nt=False):
    d = dot_nt if nt else dot
    m = a.shape[0]
    a_hi, a_lo = split2(a)
    both = d(jnp.concatenate([a_hi, a_lo], axis=0), b_hi)
    return both[:m] + (both[m:] + d(a_hi, b_lo))


def inverse_factor(m, w_ref):
    n = RANK
    lanes = lax.broadcasted_iota(jnp.int32, (1, n), 1)
    rest = m
    for p0 in range(0, n, PANEL):
        a = rest[:PANEL]
        rest = rest[PANEL:]
        below = rest
        rows = lax.broadcasted_iota(jnp.int32, (PANEL, n), 0)
        for k0 in range(0, PANEL, GROUP):
            c0 = p0 + k0
            ks = range(GROUP)
            cols = [jnp.broadcast_to(a[:, c0 + j:c0 + j + 1], (PANEL, n)) for j in ks]
            pivot = [[cols[j][k0 + i:k0 + i + 1] for j in ks] for i in ks]
            in_group = (lanes >= c0) & (lanes < c0 + GROUP)
            r = [jnp.where(in_group, jnp.where(lanes == c0 + j, 1.0, 0.0), a[k0 + j:k0 + j + 1]) for j in ks]
            inv = [None] * GROUP
            for j in ks:
                inv[j] = 1.0 / pivot[j][j]
                for i in range(j + 1, GROUP):
                    l = pivot[i][j] * inv[j]
                    r[i] = r[i] - l * r[j]
                    for t in range(j + 1, GROUP):
                        pivot[i][t] = pivot[i][t] - l * pivot[j][t]
            for j in ks:
                w_ref[c0 + j:c0 + j + 1, :] = jnp.where(lanes <= c0 + j, r[j] * lax.rsqrt(pivot[j][j]), 0.0)
            zs = [None] * GROUP
            for j in reversed(ks):
                t = r[j]
                for i in range(j + 1, GROUP):
                    t = t - pivot[j][i] * zs[i]
                zs[j] = t * inv[j]
            a = jnp.where(in_group, 0.0, a)
            for j in ks:
                a = a - cols[j] * zs[j]
            for j in ks:
                a = jnp.where(rows == k0 + j, zs[j], a)
        if p0 + PANEL < n:
            tile = p0 // 128 * 128
            width = min(128, n - tile)
            pad = [jnp.zeros((p0 - tile, n), f32)] if p0 > tile else []
            after = tile + width - p0 - PANEL
            pad_after = [jnp.zeros((after, n), f32)] if after else []
            z_hi, z_lo = split2(jnp.concatenate(pad + [a] + pad_after, axis=0))
            in_panel = (lanes >= p0) & (lanes < p0 + PANEL)
            rest = jnp.where(in_panel, 0.0, below) - dot3(below[:, tile:tile + width], z_hi, z_lo)


def iterate_kernel(d_ref, f_ref, start_ref, basis_ref, out_ref, g_hi, g_lo, q_ref, w_ref):
    g = lax.axis_index("gx")
    for i in range(G):
        for d in range(NB):
            j = (i + d) % G
            block = jnp.concatenate(
                [f_ref[i % 2, k, i // 2, 32 * d:32 * d + 32, :] for k in range(NX)], axis=0)
            hi, lo = split2(block)
            g_hi[ROWS * i:ROWS * (i + 1), ROWS * j:ROWS * (j + 1)] = hi
            g_lo[ROWS * i:ROWS * (i + 1), ROWS * j:ROWS * (j + 1)] = lo
            if 0 < d < NB - 1:
                hi, lo = split2(block.T)
                g_hi[ROWS * j:ROWS * (j + 1), ROWS * i:ROWS * (i + 1)] = hi
                g_lo[ROWS * j:ROWS * (j + 1), ROWS * i:ROWS * (i + 1)] = lo
    q_ref[...] = start_ref[...]

    def step(_, carry):
        image = dot3(q_ref[...], g_hi[...], g_lo[...])
        i_hi, i_lo = split2(image)
        both = dot_nt(jnp.concatenate([i_hi, i_lo], axis=0), i_hi)
        inner = both[:RANK] + (both[RANK:] + dot_nt(i_hi, i_lo))
        inverse_factor(inner, w_ref)
        q_ref[...] = dot3(w_ref[...], i_hi, i_lo)
        return carry

    lax.fori_loop(0, ITERS, step, 0)
    q = q_ref[...]
    d_hi, d_lo = split2(d_ref[...])
    core = dot3(q, d_hi, d_lo)
    mine_t = q_ref[:, pl.ds(pl.multiple_of(g * ROWS, ROWS), ROWS)]
    basis_ref[...] = mine_t
    mine = mine_t.T
    c_hi, c_lo = split2(core)
    out_ref[...] = dot3(mine, c_hi, c_lo)


def iterate(gathered, sums, start_t):
    cols = gathered.shape[1]
    return pl.pallas_call(
        iterate_kernel,
        out_shape=(jax.ShapeDtypeStruct((RANK, ROWS), f32), jax.ShapeDtypeStruct((ROWS, cols), f32)),
        in_specs=[pl.BlockSpec(memory_space=pltpu.VMEM)] * 3,
        out_specs=(pl.BlockSpec(memory_space=pltpu.VMEM),) * 2,
        scratch_shapes=[
            pltpu.VMEM((N, N), bf16), pltpu.VMEM((N, N), bf16),
            pltpu.VMEM((RANK, N), f32), pltpu.VMEM((RANK, RANK), f32)],
        compiler_params=pltpu.CompilerParams(vmem_limit_bytes=48 * 2**20),
    )(gathered, sums, start_t)


def body(snapshot, start):
    all_cells = snapshot.shape[1] * lax.axis_size("yz")
    gathered, sums = gather_and_gram(snapshot, all_cells)
    basis_t, projected = iterate(gathered.reshape(N, snapshot.shape[1]), sums, start.T)
    return basis_t.T, projected


def solution(mesh):
    in_specs = (P("gx", "yz"), P())
    out_specs = (P("gx", None), P("gx", "yz"))
    return jax.shard_map(body, mesh=mesh, in_specs=in_specs, out_specs=out_specs, check_vma=False)
```

```python
import functools
import jax
import jax.numpy as jnp
from jax import lax
from jax.experimental import pallas as pl
from jax.experimental.pallas import tpu as pltpu
from jax.sharding import PartitionSpec as P

ITERS = 4
G, NYH, NZ, NX, NYL, NY = 8, 4, 8, 4, 2, 8
ROWS = 128
XROWS = 176
ZROWS = 24
PAD = NZ * ZROWS
N = 1024
RANK = 192
PANEL = 32
f32, bf16 = jnp.float32, jnp.bfloat16
MESH = pl.DeviceIdType.MESH


def split2(a):
    hi = a.astype(jnp.bfloat16)
    lo = (a - hi.astype(jnp.float32)).astype(jnp.bfloat16)
    return hi, lo


def dot_nt(a, b):
    return lax.dot_general(a, b, (((1,), (1,)), ((), ())), preferred_element_type=jnp.float32)


def gram_kernel(cells, s_ref, hi_ref, lo_ref, f_ref, d_ref, parts, xin, xsum, zin, ysum, send, recv, local):
    g = lax.axis_index("gx")
    q = lax.axis_index("yz")
    yh, core = g // 2, g % 2
    z, x, yl = q // (NX * NYL), (q // NYL) % NX, q % NYL
    y = yh * NYL + yl

    def gx_at(yh2, core2):
        return (yh2 % NYH) * 2 + core2

    def yz_at(z2, x2, yl2):
        return ((z2 % NZ) * NX + x2 % NX) * NYL + yl2

    def y_peer(y2):
        return (gx_at((y2 % NY) // NYL, core), yz_at(z, x, y2 % NYL))

    def x_peer(k):
        return (g, yz_at(z, x + k, yl))

    def z_peer(k):
        return (g, yz_at(z + k, x, yl))

    pair = (gx_at(yh, 1 - core), q)
    right, left = (gx_at(yh + 1, core), q), (gx_at(yh + 3, core), q)
    peers = [pair] + [y_peer(y + k) for k in range(1, NY)]
    peers += [x_peer(k) for k in range(1, NX)] + [z_peer(k) for k in range(1, NZ)]

    barrier = pltpu.get_barrier_semaphore()
    for peer in peers:
        pl.semaphore_signal(barrier, inc=1, device_id=peer, device_id_type=MESH)
    mine = pltpu.make_async_copy(s_ref, d_ref.at[g], local)
    mine.start()
    pl.semaphore_wait(barrier, len(peers))

    sent = []
    count = [0]

    def slot(n=1):
        count[0] += n
        return count[0] - n

    def copy(src, dst, index, target):
        return pltpu.make_async_remote_copy(
            src_ref=src, dst_ref=dst, send_sem=send.at[index], recv_sem=recv.at[index],
            device_id=target, device_id_type=MESH)

    def push(ref, index, target, src=None):
        op = copy(ref if src is None else src, ref, index, target)
        op.start()
        sent.append(op)

    def arrived(ref, index):
        copy(ref, ref, index, pair).wait_recv()

    cols = s_ref.shape[1]
    half = cols // 2
    my_half = yh // 2

    def part(block, first, rows, which):
        return d_ref.at[block, pl.ds(first, rows), pl.ds(pl.multiple_of(which * half, half), half)]

    def here(block, which):
        return part(block, 0, ROWS, which)

    g_right, g_left, g_opp = right[0], left[0], gx_at(yh + 2, core)
    p_right, p_left, p_opp = (gx_at(yh + k, 1 - core) for k in (1, 3, 2))
    p_own = pair[0]
    s_pair, s_up, s_down, s_relay = slot(), slot(2), slot(2), slot(2)
    s_up2, s_relay2 = slot(), slot()
    f_right, f_opp, f_opp2, f_left, f_left2 = slot(2), slot(), slot(), slot(), slot()
    halfrows = ROWS // 2
    far = 1 - my_half

    def own(first, rows, which):
        return s_ref.at[pl.ds(first, rows), pl.ds(pl.multiple_of(which * half, half), half)]

    for c in range(2):
        push(part(g, halfrows * c, halfrows, far), s_up + c, right, own(halfrows * c, halfrows, far))
        push(here(g, c), s_down + c, left, own(0, ROWS, c))
    push(d_ref.at[g], s_pair, pair, s_ref)

    def split_into(block, which=None):
        if which is None:
            hi_ref[block], lo_ref[block] = split2(d_ref[block])
        else:
            lanes = pl.ds(pl.multiple_of(which * half, half), half)
            hi_ref[block, :, lanes], lo_ref[block, :, lanes] = split2(d_ref[block, :, lanes])

    def product(a, first, rows, b, which=None):
        lanes = slice(None) if which is None else pl.ds(pl.multiple_of(which * half, half), half)
        a_hi, a_lo = hi_ref[a, pl.ds(first, rows), lanes], lo_ref[a, pl.ds(first, rows), lanes]
        b_hi, b_lo = hi_ref[b, :, lanes], lo_ref[b, :, lanes]
        both = dot_nt(jnp.concatenate([a_hi, a_lo], axis=0), b_hi)
        return (both[:rows] + (both[rows:] + dot_nt(a_hi, b_lo))) * (1.0 / cells)

    def put(position, block):
        for k in range(NX):
            parts[k, pl.ds(pl.multiple_of(32 * position, 32), 32), :] = block[32 * k:32 * k + 32]

    mine.wait()
    split_into(g)
    put(0, product(g, 0, ROWS, g))
    arrived(d_ref.at[p_own], s_pair)
    split_into(p_own)
    block = product(gx_at(yh, 0), pl.multiple_of(halfrows * core, halfrows), halfrows, gx_at(yh, 1))
    for k in range(NX):
        parts[k, pl.ds(160, 16), :] = block[16 * k:16 * k + 16]
    for c in range(2):
        arrived(part(g_left, halfrows * c, halfrows, 1 - (yh + 3) % NYH // 2), s_up + c)
        push(part(g_left, halfrows * c, halfrows, 1 - (yh + 3) % NYH // 2), s_relay + c, right)
    for c in range(2):
        arrived(here(g_right, c), s_down + c)
        push(here(g_right, c), f_right + c, pair)
    for c in range(2):
        arrived(part(g_opp, halfrows * c, halfrows, my_half), s_relay + c)
    push(here(g_opp, my_half), f_opp, pair)
    push(here(g, my_half), s_up2, right)
    push(here(g_right, 1 - (yh + 3) % NYH // 2), s_relay2, left)
    push(here(g_left, 1 - (yh + 3) % NYH // 2), f_left, pair)
    split_into(g_right)
    put(1 + core, product(g, 0, ROWS, g_right))
    split_into(g_opp, my_half)
    put(3 + core, product(g, 0, ROWS, g_opp, my_half))
    for c in range(2):
        arrived(here(p_right, c), f_right + c)
    split_into(p_right)
    put(2 - core, product(g, 0, ROWS, p_right))
    arrived(here(p_opp, my_half), f_opp)
    split_into(p_opp, my_half)
    put(4 - core, product(g, 0, ROWS, p_opp, my_half))

    s_x = slot(NX)
    for k in range(1, NX):
        push(xin.at[k - 1], s_x + k, x_peer(k), parts.at[(x + k) % NX])
    xsum[pl.ds(XROWS, PAD - XROWS), :] = jnp.zeros((PAD - XROWS, 128), f32)
    total = parts[x]
    for k in range(1, NX):
        arrived(xin.at[k - 1], s_x + k)
        total += xin[k - 1]
    xsum[pl.ds(0, XROWS), :] = total

    def z_rows(z2):
        return pl.ds(pl.multiple_of(z2 % NZ * ZROWS, 8), ZROWS)

    s_z = slot(NZ)
    for k in range(1, NZ):
        push(zin.at[k - 1], s_z + k, z_peer(k), xsum.at[z_rows(z + k), :])
    total = xsum[z_rows(z), :]
    for k in range(1, NZ):
        arrived(zin.at[k - 1], s_z + k)
        total += zin[k - 1]
    ysum[y] = total
    s_y = slot(NY)
    for k in range(1, NY):
        push(ysum.at[y], s_y + k, y_peer(y + k))
    for k in range(1, NY):
        arrived(ysum.at[(y + k) % NY], s_y + (NY - k))
    for k in range(NYH):
        f_ref[core, x, z, k] = ysum[2 * k] + ysum[2 * k + 1]

    def slab(core2, kx, i):
        kz = (i % 2) * ((i + 1) // 2) + (1 - i % 2) * ((NZ - i // 2) % NZ)
        return f_ref.at[core2, (x + NX - kx) % NX, (z + NZ - kz) % NZ], kz

    s_az, s_right, s_left, s_far, s_ap = slot(NZ), slot(NZ), slot(NZ), slot(NZ), slot(NX * NZ)
    mine_f = f_ref.at[core, x, z]
    for i in range(1, NZ):
        kz = (i + 1) // 2 if i % 2 else NZ - i // 2
        push(mine_f, s_az + kz, z_peer(kz))

    def from_z(i, carry):
        ref, kz = slab(core, 0, i)

        @pl.when(i > 0)
        def _():
            arrived(ref, s_az + kz)

        copy(ref, ref, s_right + i, x_peer(1)).start()
        copy(ref, ref, s_left + i, x_peer(3)).start()
        copy(ref, ref, s_ap + i, pair).start()
        return carry

    lax.fori_loop(0, NZ, from_z, 0)

    def from_x(j, carry):
        for i, onward in ((2 * j, 1), (2 * j + 1, 3)):
            ref, _ = slab(core, 1, i)
            arrived(ref, s_right + i)
            if onward == 1:
                copy(ref, ref, s_far + i, x_peer(1)).start()
            copy(ref, ref, s_ap + NZ + i, pair).start()
            ref, _ = slab(core, 3, i)
            arrived(ref, s_left + i)
            if onward == 3:
                copy(ref, ref, s_far + i, x_peer(3)).start()
            copy(ref, ref, s_ap + 3 * NZ + i, pair).start()
        return carry

    lax.fori_loop(0, NZ // 2, from_x, 0)

    def from_far(i, carry):
        ref, _ = slab(core, 2, i)
        arrived(ref, s_far + i)
        copy(ref, ref, s_ap + 2 * NZ + i, pair).start()
        return carry

    lax.fori_loop(0, NZ, from_far, 0)

    left_half = (yh + 3) % NYH // 2
    arrived(here(g_left, left_half), s_up2)
    push(here(g_left, left_half), f_left2, pair)
    arrived(here(g_opp, far), s_relay2)
    push(here(g_opp, far), f_opp2, pair)
    split_into(g_left)
    split_into(g_opp, far)
    arrived(here(p_left, 1 - left_half), f_left)
    arrived(here(p_left, left_half), f_left2)
    split_into(p_left)
    arrived(here(p_opp, far), f_opp2)
    split_into(p_opp, far)

    def finish(i, carry):
        ref, _ = slab(core, 0, i)
        copy(ref, ref, s_right + i, x_peer(1)).wait_send()
        copy(ref, ref, s_left + i, x_peer(3)).wait_send()
        copy(ref, ref, s_far + i, x_peer(1)).wait_send()
        for kx in range(NX):
            ref, _ = slab(1 - core, kx, i)
            arrived(ref, s_ap + kx * NZ + i)
            copy(ref, ref, s_ap + kx * NZ + i, pair).wait_send()
        return carry

    lax.fori_loop(0, NZ, finish, 0)
    for op in sent:
        op.wait_send()


SLOTS = 1 + 2 + 2 + 2 + 2 + 6 + NX + NZ + NY + 4 * NZ + NX * NZ


def gather_and_gram(snapshot, all_cells):
    cols = snapshot.shape[1]
    vmem = pl.BlockSpec(memory_space=pltpu.VMEM)
    return pl.pallas_call(
        functools.partial(gram_kernel, all_cells),
        out_shape=(jax.ShapeDtypeStruct((G, ROWS, cols), bf16),
                   jax.ShapeDtypeStruct((G, ROWS, cols), bf16),
                   jax.ShapeDtypeStruct((2, NX, NZ, NYH, ZROWS, 128), f32)),
        in_specs=[vmem],
        out_specs=(vmem, vmem, vmem),
        scratch_shapes=[
            pltpu.VMEM((G, ROWS, cols), f32),
            pltpu.VMEM((NX, XROWS, 128), f32),
            pltpu.VMEM((NX - 1, XROWS, 128), f32),
            pltpu.VMEM((PAD, 128), f32),
            pltpu.VMEM((NZ - 1, ZROWS, 128), f32),
            pltpu.VMEM((NY, ZROWS, 128), f32),
            pltpu.SemaphoreType.DMA((SLOTS,)),
            pltpu.SemaphoreType.DMA((SLOTS,)),
            pltpu.SemaphoreType.DMA,
        ],
        compiler_params=pltpu.CompilerParams(
            collective_id=0, has_side_effects=True, vmem_limit_bytes=28 * 2**20),
    )(snapshot)


def dot(a, b):
    return lax.dot_general(a, b, (((1,), (0,)), ((), ())), preferred_element_type=f32)


def dot3(a, b_hi, b_lo, nt=False):
    d = dot_nt if nt else dot
    m = a.shape[0]
    a_hi, a_lo = split2(a)
    both = d(jnp.concatenate([a_hi, a_lo], axis=0), b_hi)
    return both[:m] + (both[m:] + d(a_hi, b_lo))


def reciprocal(x):
    r = pl.reciprocal(x, approx=True)
    return r * (2.0 - x * r)


def inverse_factor(m, w_ref):
    n = RANK
    lane = lax.broadcasted_iota(jnp.int32, (8, 128), 1)
    row = lax.broadcasted_iota(jnp.int32, (8, 128), 0)
    js = range(8)
    full = lambda v: jnp.broadcast_to(v, (8, 128))

    def stack(rows):
        t = rows[0]
        for j in js[1:]:
            t = jnp.where(row == j, rows[j], t)
        return t

    rest = jnp.concatenate([m, jnp.zeros((n, 256 - n), f32)], axis=1)
    for p0 in range(0, n, PANEL):
        tiles = [[rest[8 * i:8 * i + 8, 128 * h:128 * h + 128] for h in range(2)] for i in range(PANEL // 8)]
        below = rest[PANEL:]
        ct = p0 // 128
        for gi in range(PANEL // 8):
            c0 = p0 + 8 * gi
            cl = c0 - 128 * ct
            here = (lane >= cl) & (lane < cl + 8)
            t = tiles[gi]
            piv = [[None] * 8 for _ in js]
            for j in js:
                col = full(t[ct][:, cl + j:cl + j + 1])
                for i in range(j + 1):
                    piv[i][j] = full(col[i:i + 1])
            r = [[full(t[h][j:j + 1]) for h in range(2)] for j in js]
            for j in js:
                r[j][ct] = jnp.where(here, jnp.where(lane == cl + j, 1.0, 0.0), r[j][ct])
            inv = [None] * 8
            for j in js:
                inv[j] = reciprocal(piv[j][j])
                for i in range(j + 1, 8):
                    l = piv[j][i] * inv[j]
                    for k in range(i, 8):
                        piv[i][k] = piv[i][k] - l * piv[j][k]
                    for h in range(2):
                        r[i][h] = r[i][h] - l * r[j][h]
            for h in range(2):
                w = stack([r[j][h] * lax.rsqrt(piv[j][j]) for j in js])
                w_ref[c0:c0 + 8, 128 * h:128 * h + 128] = jnp.where(lane + 128 * h <= row + c0, w, 0.0)
            z = [None] * 8
            for j in reversed(js):
                z[j] = []
                for h in range(2):
                    v = r[j][h]
                    for i in range(7, j, -1):
                        v = v - piv[j][i] * z[i][h]
                    z[j].append(v * inv[j])
            for i in range(PANEL // 8):
                if i == gi:
                    continue
                cols = [full(tiles[i][ct][:, cl + j:cl + j + 1]) for j in js]
                old = tiles[i]
                tiles[i] = []
                for h in range(2):
                    v = jnp.where(here, 0.0, old[h]) if h == ct else old[h]
                    even = sum(cols[j] * z[j][h] for j in js[0::2])
                    odd = sum(cols[j] * z[j][h] for j in js[1::2])
                    tiles[i].append(v - (even + odd))
            tiles[gi] = [stack([z[j][h] for j in js]) for h in range(2)]
        if p0 + PANEL < n:
            a = jnp.concatenate([jnp.concatenate(t, axis=1) for t in tiles], axis=0)
            parts = [a]
            if p0 > 128 * ct:
                parts = [jnp.zeros((p0 - 128 * ct, 256), f32)] + parts
            after = 128 * ct + 128 - p0 - PANEL
            if after:
                parts = parts + [jnp.zeros((after, 256), f32)]
            z_hi, z_lo = split2(jnp.concatenate(parts, axis=0))
            lanes = lax.broadcasted_iota(jnp.int32, (1, 256), 1)
            in_panel = (lanes >= p0) & (lanes < p0 + PANEL)
            rest = jnp.where(in_panel, 0.0, below) - dot3(below[:, 128 * ct:128 * ct + 128], z_hi, z_lo)


def iterate_kernel(hi_ref, lo_ref, f_ref, start_ref, basis_ref, out_ref, g_hi, g_lo, i_ref, w_ref):
    g = lax.axis_index("gx")

    def store(i, j, block):
        hi, lo = split2(block)
        g_hi[ROWS * i:ROWS * (i + 1), ROWS * j:ROWS * (j + 1)] = hi
        g_lo[ROWS * i:ROWS * (i + 1), ROWS * j:ROWS * (j + 1)] = lo

    def rows(i, first, count):
        own = [f_ref[i % 2, k, :, i // 2].reshape(PAD, 128)[first:first + count] for k in range(NX)]
        return jnp.concatenate(own, axis=0)

    for yh in range(NYH):
        a, b = 2 * yh, 2 * yh + 1
        pair = jnp.concatenate([rows(a, 160, 16), rows(b, 160, 16)], axis=0)
        store(a, b, pair)
        store(b, a, pair.T)
        for i in (a, b):
            store(i, i, rows(i, 0, 32))
            for c in range(2):
                j = 2 * ((yh + 1) % NYH) + c
                block = rows(i, 32 * (1 + c), 32)
                store(i, j, block)
                store(j, i, block.T)
                j = 2 * ((yh + 2) % NYH) + c
                if yh < 2:
                    block = rows(i, 32 * (3 + c), 32) + rows(j, 32 * (3 + i % 2), 32).T
                    store(i, j, block)
                    store(j, i, block.T)
    i_ref[...] = dot3(start_ref[...], g_hi[...], g_lo[...])

    def factor(i_hi, i_lo):
        both = dot_nt(jnp.concatenate([i_hi, i_lo], axis=0), i_hi)
        inverse_factor(both[:RANK] + (both[RANK:] + dot_nt(i_hi, i_lo)), w_ref)

    def times(i_hi, i_lo, b_hi, b_lo):
        both = dot(jnp.concatenate([i_hi, i_lo], axis=0), b_hi)
        return both[:RANK] + (both[RANK:] + dot(i_hi, b_lo))

    def step(_, carry):
        i_hi, i_lo = split2(i_ref[...])
        after = times(i_hi, i_lo, g_hi[...], g_lo[...])
        factor(i_hi, i_lo)
        i_ref[...] = dot3(w_ref[:, :RANK], *split2(after))
        return carry

    lax.fori_loop(0, ITERS - 1, step, 0)
    i_hi, i_lo = split2(i_ref[...])
    after = times(i_hi, i_lo, hi_ref[...], lo_ref[...])
    factor(i_hi, i_lo)
    w = w_ref[:, :RANK]
    core = dot3(w, *split2(after))
    mine_t = dot3(w, *split2(i_ref[:, pl.ds(pl.multiple_of(g * ROWS, ROWS), ROWS)]))
    basis_ref[...] = mine_t
    out_ref[...] = dot3(mine_t.T, *split2(core))


def iterate(d_hi, d_lo, sums, start_t):
    cols = d_hi.shape[1]
    vmem = pl.BlockSpec(memory_space=pltpu.VMEM)
    return pl.pallas_call(
        iterate_kernel,
        out_shape=(jax.ShapeDtypeStruct((RANK, ROWS), f32), jax.ShapeDtypeStruct((ROWS, cols), f32)),
        in_specs=[vmem] * 4,
        out_specs=(vmem, vmem),
        scratch_shapes=[
            pltpu.VMEM((N, N), bf16), pltpu.VMEM((N, N), bf16),
            pltpu.VMEM((RANK, N), f32), pltpu.VMEM((RANK, 256), f32)],
        compiler_params=pltpu.CompilerParams(vmem_limit_bytes=28 * 2**20),
    )(d_hi, d_lo, sums, start_t)


def body(snapshot, start):
    all_cells = snapshot.shape[1] * lax.axis_size("yz")
    d_hi, d_lo, sums = gather_and_gram(snapshot, all_cells)
    shape = (N, snapshot.shape[1])
    basis_t, projected = iterate(d_hi.reshape(shape), d_lo.reshape(shape), sums, start.T)
    return basis_t.T, projected


def solution(mesh):
    in_specs = (P("gx", "yz"), P())
    out_specs = (P("gx", None), P("gx", "yz"))
    return jax.shard_map(body, mesh=mesh, in_specs=in_specs, out_specs=out_specs, check_vma=False)
```

```python
import functools
import jax
import jax.numpy as jnp
from jax import lax
from jax.experimental import pallas as pl
from jax.experimental.pallas import tpu as pltpu
from jax.sharding import PartitionSpec as P

ITERS = 4
G, NYH, NZ, NX, NYL, NY = 8, 4, 8, 4, 2, 8
ROWS = 128
KINDS = 4
N = 1024
RANK = 192
PANEL = 32
f32, bf16 = jnp.float32, jnp.bfloat16
MESH = pl.DeviceIdType.MESH


def split2(a):
    hi = a.astype(jnp.bfloat16)
    lo = (a - hi.astype(jnp.float32)).astype(jnp.bfloat16)
    return hi, lo


def dot_nt(a, b):
    return lax.dot_general(a, b, (((1,), (1,)), ((), ())), preferred_element_type=jnp.float32)


def gram_kernel(cells, s_ref, hi_ref, lo_ref, f_ref, d_ref, parts, xin, xsum, zin, ysum, send, recv, local):
    g = lax.axis_index("gx")
    q = lax.axis_index("yz")
    yh, core = g // 2, g % 2
    z, x, yl = q // (NX * NYL), (q // NYL) % NX, q % NYL
    y = yh * NYL + yl

    def gx_at(yh2, core2):
        return (yh2 % NYH) * 2 + core2

    def yz_at(z2, x2, yl2):
        return ((z2 % NZ) * NX + x2 % NX) * NYL + yl2

    def y_peer(y2):
        return (gx_at((y2 % NY) // NYL, core), yz_at(z, x, y2 % NYL))

    def x_peer(k):
        return (g, yz_at(z, x + k, yl))

    def z_peer(k):
        return (g, yz_at(z + k, x, yl))

    pair = (gx_at(yh, 1 - core), q)
    right, left = (gx_at(yh + 1, core), q), (gx_at(yh + 3, core), q)
    peers = [pair] + [y_peer(y + k) for k in range(1, NY)]
    peers += [x_peer(k) for k in range(1, NX)] + [z_peer(k) for k in range(1, NZ)]

    barrier = pltpu.get_barrier_semaphore()
    for peer in peers:
        pl.semaphore_signal(barrier, inc=1, device_id=peer, device_id_type=MESH)
    mine = pltpu.make_async_copy(s_ref, d_ref.at[g], local)
    mine.start()
    pl.semaphore_wait(barrier, len(peers))

    sent = []
    count = [0]

    def slot(n=1):
        count[0] += n
        return count[0] - n

    def copy(src, dst, index, target):
        return pltpu.make_async_remote_copy(
            src_ref=src, dst_ref=dst, send_sem=send.at[index], recv_sem=recv.at[index],
            device_id=target, device_id_type=MESH)

    def push(ref, index, target, src=None):
        op = copy(ref if src is None else src, ref, index, target)
        op.start()
        sent.append(op)

    def arrived(ref, index):
        copy(ref, ref, index, pair).wait_recv()

    quarter = s_ref.shape[1] // 4
    mine_q = yh // 2
    far_q = 1 - mine_q
    right_q = 1 - (yh + 1) % NYH // 2
    left_q = 1 - (yh + 3) % NYH // 2

    def lanes(first, n):
        return pl.ds(pl.multiple_of(first * quarter, quarter), n * quarter)

    def cells_of(block, first, n=1):
        return d_ref.at[block, :, lanes(first, n)]

    def own(first, n=1):
        return s_ref.at[:, lanes(first, n)]

    g_right, g_left, g_opp = right[0], left[0], gx_at(yh + 2, core)
    p_own = pair[0]
    p_right, p_left, p_opp = (gx_at(yh + k, 1 - core) for k in (1, 3, 2))
    s_pair, s_down, s_up, s_relay = slot(), slot(2), slot(2), slot(2)
    f_right, f_left, f_opp = slot(2), slot(2), slot(2)
    push(cells_of(g, far_q), s_down, left, own(far_q))
    push(cells_of(g, 2 + far_q), s_up, right, own(2 + far_q))
    push(d_ref.at[g], s_pair, pair, s_ref)
    push(cells_of(g, mine_q), s_down + 1, left, own(mine_q))
    push(cells_of(g, 2 + mine_q), s_up + 1, right, own(2 + mine_q))

    def split_into(block, first, n):
        where = lanes(first, n)
        hi_ref[block, :, where], lo_ref[block, :, where] = split2(d_ref[block, :, where])

    def product(a, b, segments, first=0, rows=ROWS):
        total = None
        for begin, n in segments:
            where = lanes(begin, n)
            a_hi, a_lo = hi_ref[a, pl.ds(first, rows), where], lo_ref[a, pl.ds(first, rows), where]
            b_hi, b_lo = hi_ref[b, :, where], lo_ref[b, :, where]
            both = dot_nt(jnp.concatenate([a_hi, a_lo], axis=0), b_hi)
            term = both[:rows] + (both[rows:] + dot_nt(a_hi, b_lo))
            total = term if total is None else total + term
        return total * (1.0 / cells)

    def put(kind, position, block):
        rows = block.shape[0] // NX
        for k in range(NX):
            parts[k, kind, position:position + rows // 8] = block[rows * k:rows * (k + 1)].reshape(rows // 8, 8, 128)

    class Sums:
        def __init__(self, lo, n):
            self.kinds = pl.ds(lo, n)
            self.x, self.z, self.y = slot(NX), slot(NZ), slot(NY)

        def send_x(self):
            for k in range(1, NX):
                push(xin.at[k - 1, self.kinds], self.x + k, x_peer(k), parts.at[(x + k) % NX, self.kinds])

        def send_z(self):
            total = parts[x, self.kinds]
            for k in range(1, NX):
                arrived(xin.at[k - 1, self.kinds], self.x + k)
                total += xin[k - 1, self.kinds]
            xsum[self.kinds] = total
            for k in range(1, NZ):
                push(zin.at[k - 1, self.kinds], self.z + k, z_peer(k), xsum.at[self.kinds, (z + k) % NZ])

        def send_y(self):
            total = xsum[self.kinds, z]
            for k in range(1, NZ):
                arrived(zin.at[k - 1, self.kinds], self.z + k)
                total += zin[k - 1, self.kinds]
            ysum[y, self.kinds] = total
            for k in range(1, NY):
                push(ysum.at[y, self.kinds], self.y + k, y_peer(y + k))

        def finish(self):
            for k in range(1, NY):
                arrived(ysum.at[(y + NY - k) % NY, self.kinds], self.y + k)

    class Spread:
        def __init__(self, lo, n):
            self.tiles = pl.ds(lo, n)
            self.z, self.x, self.pair = slot(NZ), slot(NX), slot(NX)

        def part(self, core2, k):
            return f_ref.at[core2, (x + NX - k) % NX, :, self.tiles]

        def send_z(self):
            for k in (1, 7, 2, 6, 3, 5, 4):
                push(f_ref.at[core, x, z, self.tiles], self.z + k, z_peer(k))

        def send_x(self):
            for k in range(1, NZ):
                arrived(f_ref.at[core, x, (z + NZ - k) % NZ, self.tiles], self.z + k)
            for k in (2, 1, 3):
                push(self.part(core, 0), self.x + k, x_peer(k))
            push(self.part(core, 0), self.pair, pair)

        def send_pair(self):
            for k in (1, 3, 2):
                arrived(self.part(core, k), self.x + k)
                push(self.part(core, k), self.pair + k, pair)

        def finish(self):
            for k in range(NX):
                arrived(self.part(1 - core, k), self.pair + k)

    sum_own, sum_near, sum_opp = Sums(0, 1), Sums(1, 2), Sums(3, 1)
    all_own, all_near, all_opp = Spread(0, NYH), Spread(NYH, NYH), Spread(2 * NYH, 2)

    mine.wait()
    split_into(g, 0, 4)
    put(0, 0, product(g, g, [(0, 4)]))
    arrived(d_ref.at[p_own], s_pair)
    split_into(p_own, 0, 4)
    halfrows = ROWS // 2
    first = pl.multiple_of(halfrows * core, halfrows)
    put(0, 4, product(gx_at(yh, 0), gx_at(yh, 1), [(0, 4)], first, halfrows))
    for k in range(NX):
        parts[k, 0, 6:8] = jnp.zeros((2, 8, 128), f32)
    sum_own.send_x()

    arrived(cells_of(g_right, right_q), s_down)
    push(cells_of(g_right, right_q), s_relay, left)
    push(cells_of(g_right, right_q), f_right, pair)
    arrived(cells_of(g_left, 2 + left_q), s_up)
    push(cells_of(g_left, 2 + left_q), s_relay + 1, right)
    push(cells_of(g_left, 2 + left_q), f_left, pair)
    sum_own.send_z()
    arrived(cells_of(g_right, 1 - right_q), s_down + 1)
    push(cells_of(g_right, 1 - right_q), f_right + 1, pair)
    arrived(cells_of(g_left, 3 - left_q), s_up + 1)
    push(cells_of(g_left, 3 - left_q), f_left + 1, pair)
    sum_own.send_y()
    split_into(g_right, 0, 2)
    split_into(g_left, 2, 2)
    arrived(cells_of(p_right, right_q), f_right)
    arrived(cells_of(p_right, 1 - right_q), f_right + 1)
    split_into(p_right, 0, 2)
    for c in range(2):
        put(1, 4 * c, product(g, gx_at(yh + 1, c), [(0, 2)]))
        put(2, 4 * c, product(g_left, gx_at(yh, c), [(2, 2)]))
    sum_near.send_x()
    sum_own.finish()
    for k in range(NYH):
        f_ref[core, x, z, k] = ysum[2 * k, 0] + ysum[2 * k + 1, 0]
    all_own.send_z()

    arrived(cells_of(g_opp, mine_q), s_relay)
    push(cells_of(g_opp, mine_q), f_opp, pair)
    arrived(cells_of(g_opp, 2 + mine_q), s_relay + 1)
    push(cells_of(g_opp, 2 + mine_q), f_opp + 1, pair)
    l_right, l_left, l_relay, l_pair = slot(), slot(), slot(2), slot(4)
    push(cells_of(g_right, 1 - right_q), l_relay, left)
    push(cells_of(g_left, 3 - left_q), l_relay + 1, right)
    push(cells_of(g, 0, 2), l_right, right, own(0, 2))
    push(cells_of(g, 2, 2), l_left, left, own(2, 2))
    split_into(g_opp, mine_q, 1)
    split_into(g_opp, 2 + mine_q, 1)
    sum_near.send_z()
    arrived(cells_of(p_opp, mine_q), f_opp)
    split_into(p_opp, mine_q, 1)
    arrived(cells_of(p_opp, 2 + mine_q), f_opp + 1)
    split_into(p_opp, 2 + mine_q, 1)
    for c in range(2):
        put(3, 4 * c, product(gx_at(yh % 2, core), gx_at(yh % 2 + 2, c), [(mine_q, 1), (2 + mine_q, 1)]))
    sum_opp.send_x()
    all_own.send_x()
    sum_near.send_y()
    sum_opp.send_z()
    sum_near.finish()
    for k in range(NYH):
        after = (k + 1) % NYH
        f_ref[core, x, z, NYH + k] = (ysum[2 * k, 1] + ysum[2 * k + 1, 1]) + (ysum[2 * after, 2] + ysum[2 * after + 1, 2])
    all_near.send_z()
    sum_opp.send_y()
    all_own.send_pair()
    sum_opp.finish()
    for k in range(2):
        f_ref[core, x, z, 2 * NYH + k] = (ysum[2 * k, 3] + ysum[2 * k + 1, 3]) + (ysum[2 * k + 4, 3] + ysum[2 * k + 5, 3])
    all_opp.send_z()
    all_near.send_x()
    all_opp.send_x()
    arrived(cells_of(g_opp, far_q), l_relay)
    push(cells_of(g_opp, far_q), l_pair, pair)
    arrived(cells_of(g_opp, 2 + far_q), l_relay + 1)
    push(cells_of(g_opp, 2 + far_q), l_pair + 1, pair)
    split_into(g_opp, far_q, 1)
    split_into(g_opp, 2 + far_q, 1)
    arrived(cells_of(p_left, 2 + left_q), f_left)
    arrived(cells_of(p_left, 3 - left_q), f_left + 1)
    split_into(p_left, 2, 2)
    all_near.send_pair()
    all_opp.send_pair()
    arrived(cells_of(g_left, 0, 2), l_right)
    push(cells_of(g_left, 0, 2), l_pair + 2, pair)
    arrived(cells_of(g_right, 2, 2), l_left)
    push(cells_of(g_right, 2, 2), l_pair + 3, pair)
    split_into(g_left, 0, 2)
    split_into(g_right, 2, 2)
    arrived(cells_of(p_opp, far_q), l_pair)
    split_into(p_opp, far_q, 1)
    arrived(cells_of(p_opp, 2 + far_q), l_pair + 1)
    split_into(p_opp, 2 + far_q, 1)
    arrived(cells_of(p_left, 0, 2), l_pair + 2)
    split_into(p_left, 0, 2)
    arrived(cells_of(p_right, 2, 2), l_pair + 3)
    split_into(p_right, 2, 2)
    for group in (all_own, all_near, all_opp):
        group.finish()
    for op in sent:
        op.wait_send()


TILES = 2 * NYH + 2
SLOTS = 13 + 8 + 3 * (NX + NZ + NY) + 3 * (NZ + 2 * NX)


def gather_and_gram(snapshot, all_cells):
    cols = snapshot.shape[1]
    vmem = pl.BlockSpec(memory_space=pltpu.VMEM)
    return pl.pallas_call(
        functools.partial(gram_kernel, all_cells),
        out_shape=(jax.ShapeDtypeStruct((G, ROWS, cols), bf16),
                   jax.ShapeDtypeStruct((G, ROWS, cols), bf16),
                   jax.ShapeDtypeStruct((2, NX, NZ, TILES, 8, 128), f32)),
        in_specs=[vmem],
        out_specs=(vmem, vmem, vmem),
        scratch_shapes=[
            pltpu.VMEM((G, ROWS, cols), f32),
            pltpu.VMEM((NX, KINDS, NZ, 8, 128), f32),
            pltpu.VMEM((NX - 1, KINDS, NZ, 8, 128), f32),
            pltpu.VMEM((KINDS, NZ, 8, 128), f32),
            pltpu.VMEM((NZ - 1, KINDS, 8, 128), f32),
            pltpu.VMEM((NY, KINDS, 8, 128), f32),
            pltpu.SemaphoreType.DMA((SLOTS,)),
            pltpu.SemaphoreType.DMA((SLOTS,)),
            pltpu.SemaphoreType.DMA,
        ],
        compiler_params=pltpu.CompilerParams(
            collective_id=0, has_side_effects=True, vmem_limit_bytes=28 * 2**20),
    )(snapshot)


def dot(a, b):
    return lax.dot_general(a, b, (((1,), (0,)), ((), ())), preferred_element_type=f32)


def dot3(a, b_hi, b_lo, nt=False):
    d = dot_nt if nt else dot
    m = a.shape[0]
    a_hi, a_lo = split2(a)
    both = d(jnp.concatenate([a_hi, a_lo], axis=0), b_hi)
    return both[:m] + (both[m:] + d(a_hi, b_lo))


def reciprocal(x):
    r = pl.reciprocal(x, approx=True)
    return r * (2.0 - x * r)


def inverse_factor(m, w_ref):
    n = RANK
    lane = lax.broadcasted_iota(jnp.int32, (8, 128), 1)
    row = lax.broadcasted_iota(jnp.int32, (8, 128), 0)
    js = range(8)
    full = lambda v: jnp.broadcast_to(v, (8, 128))

    def stack(rows):
        t = rows[0]
        for j in js[1:]:
            t = jnp.where(row == j, rows[j], t)
        return t

    rest = jnp.concatenate([m, jnp.zeros((n, 256 - n), f32)], axis=1)
    for p0 in range(0, n, PANEL):
        tiles = [[rest[8 * i:8 * i + 8, 128 * h:128 * h + 128] for h in range(2)] for i in range(PANEL // 8)]
        below = rest[PANEL:]
        ct = p0 // 128
        for gi in range(PANEL // 8):
            c0 = p0 + 8 * gi
            cl = c0 - 128 * ct
            here = (lane >= cl) & (lane < cl + 8)
            t = tiles[gi]
            piv = [[None] * 8 for _ in js]
            for j in js:
                col = full(t[ct][:, cl + j:cl + j + 1])
                for i in range(j + 1):
                    piv[i][j] = full(col[i:i + 1])
            r = [[full(t[h][j:j + 1]) for h in range(2)] for j in js]
            for j in js:
                r[j][ct] = jnp.where(here, jnp.where(lane == cl + j, 1.0, 0.0), r[j][ct])
            inv = [None] * 8
            for j in js:
                inv[j] = reciprocal(piv[j][j])
                for i in range(j + 1, 8):
                    l = piv[j][i] * inv[j]
                    for k in range(i, 8):
                        piv[i][k] = piv[i][k] - l * piv[j][k]
                    for h in range(2):
                        r[i][h] = r[i][h] - l * r[j][h]
            for h in range(2):
                w = stack([r[j][h] * lax.rsqrt(piv[j][j]) for j in js])
                w_ref[c0:c0 + 8, 128 * h:128 * h + 128] = jnp.where(lane + 128 * h <= row + c0, w, 0.0)
            z = [None] * 8
            for j in reversed(js):
                z[j] = []
                for h in range(2):
                    v = r[j][h]
                    for i in range(7, j, -1):
                        v = v - piv[j][i] * z[i][h]
                    z[j].append(v * inv[j])
            for i in range(PANEL // 8):
                if i == gi:
                    continue
                cols = [full(tiles[i][ct][:, cl + j:cl + j + 1]) for j in js]
                old = tiles[i]
                tiles[i] = []
                for h in range(2):
                    v = jnp.where(here, 0.0, old[h]) if h == ct else old[h]
                    even = sum(cols[j] * z[j][h] for j in js[0::2])
                    odd = sum(cols[j] * z[j][h] for j in js[1::2])
                    tiles[i].append(v - (even + odd))
            tiles[gi] = [stack([z[j][h] for j in js]) for h in range(2)]
        if p0 + PANEL < n:
            a = jnp.concatenate([jnp.concatenate(t, axis=1) for t in tiles], axis=0)
            parts = [a]
            if p0 > 128 * ct:
                parts = [jnp.zeros((p0 - 128 * ct, 256), f32)] + parts
            after = 128 * ct + 128 - p0 - PANEL
            if after:
                parts = parts + [jnp.zeros((after, 256), f32)]
            z_hi, z_lo = split2(jnp.concatenate(parts, axis=0))
            lanes = lax.broadcasted_iota(jnp.int32, (1, 256), 1)
            in_panel = (lanes >= p0) & (lanes < p0 + PANEL)
            rest = jnp.where(in_panel, 0.0, below) - dot3(below[:, 128 * ct:128 * ct + 128], z_hi, z_lo)


def iterate_kernel(hi_ref, lo_ref, f_ref, start_ref, basis_ref, out_ref, g_hi, g_lo, i_ref, w_ref):
    g = lax.axis_index("gx")


    def store(i, j, block):
        hi, lo = split2(block)
        g_hi[ROWS * i:ROWS * (i + 1), ROWS * j:ROWS * (j + 1)] = hi
        g_lo[ROWS * i:ROWS * (i + 1), ROWS * j:ROWS * (j + 1)] = lo

    def rows(core, tile, first, count):
        own = [f_ref[core, k, :, tile].reshape(NZ * 8, 128)[first:first + count] for k in range(NX)]
        return jnp.concatenate(own, axis=0)

    for yh in range(NYH):
        a, b = 2 * yh, 2 * yh + 1
        pair = jnp.concatenate([rows(0, yh, 32, 16), rows(1, yh, 32, 16)], axis=0)
        store(a, b, pair)
        store(b, a, pair.T)
        for core in range(2):
            i = 2 * yh + core
            store(i, i, rows(core, yh, 0, 32))
            for c in range(2):
                j = 2 * ((yh + 1) % NYH) + c
                block = rows(core, NYH + yh, 32 * c, 32)
                store(i, j, block)
                store(j, i, block.T)
                if yh < 2:
                    j = 2 * (yh + 2) + c
                    block = rows(core, 2 * NYH + yh, 32 * c, 32)
                    store(i, j, block)
                    store(j, i, block.T)

    i_ref[...] = dot3(start_ref[...], g_hi[...], g_lo[...])

    def factor(i_hi, i_lo):
        both = dot_nt(jnp.concatenate([i_hi, i_lo], axis=0), i_hi)
        inverse_factor(both[:RANK] + (both[RANK:] + dot_nt(i_hi, i_lo)), w_ref)

    def times(i_hi, i_lo, b_hi, b_lo):
        both = dot(jnp.concatenate([i_hi, i_lo], axis=0), b_hi)
        return both[:RANK] + (both[RANK:] + dot(i_hi, b_lo))

    def step(_, carry):
        i_hi, i_lo = split2(i_ref[...])
        after = times(i_hi, i_lo, g_hi[...], g_lo[...])
        factor(i_hi, i_lo)
        i_ref[...] = dot3(w_ref[:, :RANK], *split2(after))
        return carry

    lax.fori_loop(0, ITERS - 1, step, 0)
    i_hi, i_lo = split2(i_ref[...])
    after = times(i_hi, i_lo, hi_ref[...], lo_ref[...])
    factor(i_hi, i_lo)
    w = w_ref[:, :RANK]
    core = dot3(w, *split2(after))
    mine_t = dot3(w, *split2(i_ref[:, pl.ds(pl.multiple_of(g * ROWS, ROWS), ROWS)]))
    basis_ref[...] = mine_t
    out_ref[...] = dot3(mine_t.T, *split2(core))


def iterate(d_hi, d_lo, sums, start_t):
    cols = d_hi.shape[1]
    vmem = pl.BlockSpec(memory_space=pltpu.VMEM)
    return pl.pallas_call(
        iterate_kernel,
        out_shape=(jax.ShapeDtypeStruct((RANK, ROWS), f32), jax.ShapeDtypeStruct((ROWS, cols), f32)),
        in_specs=[vmem] * 4,
        out_specs=(vmem, vmem),
        scratch_shapes=[
            pltpu.VMEM((N, N), bf16), pltpu.VMEM((N, N), bf16),
            pltpu.VMEM((RANK, N), f32), pltpu.VMEM((RANK, 256), f32)],
        compiler_params=pltpu.CompilerParams(vmem_limit_bytes=28 * 2**20),
    )(d_hi, d_lo, sums, start_t)


def body(snapshot, start):
    all_cells = snapshot.shape[1] * lax.axis_size("yz")
    d_hi, d_lo, sums = gather_and_gram(snapshot, all_cells)
    shape = (N, snapshot.shape[1])
    basis_t, projected = iterate(d_hi.reshape(shape), d_lo.reshape(shape), sums, start.T)
    return basis_t.T, projected


def solution(mesh):
    in_specs = (P("gx", "yz"), P())
    out_specs = (P("gx", None), P("gx", "yz"))
    return jax.shard_map(body, mesh=mesh, in_specs=in_specs, out_specs=out_specs, check_vma=False)
```

```python
import functools
import jax
import jax.numpy as jnp
from jax import lax
from jax.experimental import pallas as pl
from jax.experimental.pallas import tpu as pltpu
from jax.sharding import PartitionSpec as P

ITERS = 4
G, NYH, NZ, NX, NYL, NY = 8, 4, 8, 4, 2, 8
ROWS = 128
KINDS = 4
RING_ORDER = (4, 3, 5, 2, 6, 1, 7)
N = 1024
RANK = 192
PANEL = 32
f32, bf16 = jnp.float32, jnp.bfloat16
MESH = pl.DeviceIdType.MESH


def split2(a):
    hi = a.astype(jnp.bfloat16)
    lo = (a - hi.astype(jnp.float32)).astype(jnp.bfloat16)
    return hi, lo


def dot_nt(a, b):
    return lax.dot_general(a, b, (((1,), (1,)), ((), ())), preferred_element_type=jnp.float32)


def gram_kernel(cells, s_ref, hi_ref, lo_ref, f_ref, d_ref, parts, xin, xsum, zin, ysum, send, recv, local):
    g = lax.axis_index("gx")
    q = lax.axis_index("yz")
    yh, core = g // 2, g % 2
    z, x, yl = q // (NX * NYL), (q // NYL) % NX, q % NYL
    y = yh * NYL + yl

    def gx_at(yh2, core2):
        return (yh2 % NYH) * 2 + core2

    def yz_at(z2, x2, yl2):
        return ((z2 % NZ) * NX + x2 % NX) * NYL + yl2

    def y_peer(y2):
        return (gx_at((y2 % NY) // NYL, core), yz_at(z, x, y2 % NYL))

    def x_peer(k):
        return (g, yz_at(z, x + k, yl))

    def z_peer(k):
        return (g, yz_at(z + k, x, yl))

    pair = (gx_at(yh, 1 - core), q)
    right, left = (gx_at(yh + 1, core), q), (gx_at(yh + 3, core), q)
    peers = [pair] + [y_peer(y + k) for k in range(1, NY)]
    peers += [x_peer(k) for k in range(1, NX)] + [z_peer(k) for k in range(1, NZ)]

    barrier = pltpu.get_barrier_semaphore()
    for peer in peers:
        pl.semaphore_signal(barrier, inc=1, device_id=peer, device_id_type=MESH)
    mine = pltpu.make_async_copy(s_ref, d_ref.at[g], local)
    mine.start()
    pl.semaphore_wait(barrier, len(peers))

    sent = []
    count = [0]

    def slot(n=1):
        count[0] += n
        return count[0] - n

    def copy(src, dst, index, target):
        return pltpu.make_async_remote_copy(
            src_ref=src, dst_ref=dst, send_sem=send.at[index], recv_sem=recv.at[index],
            device_id=target, device_id_type=MESH)

    def push(ref, index, target, src=None):
        op = copy(ref if src is None else src, ref, index, target)
        op.start()
        sent.append(op)

    def arrived(ref, index):
        copy(ref, ref, index, pair).wait_recv()

    quarter = s_ref.shape[1] // 4
    mine_q = yh // 2
    far_q = 1 - mine_q
    right_q = 1 - (yh + 1) % NYH // 2
    left_q = 1 - (yh + 3) % NYH // 2

    def lanes(first, n):
        return pl.ds(pl.multiple_of(first * quarter, quarter), n * quarter)

    def cells_of(block, first, n=1):
        return d_ref.at[block, :, lanes(first, n)]

    def own(first, n=1):
        return s_ref.at[:, lanes(first, n)]

    g_right, g_left, g_opp = right[0], left[0], gx_at(yh + 2, core)
    p_own = pair[0]
    p_right, p_left, p_opp = (gx_at(yh + k, 1 - core) for k in (1, 3, 2))
    s_pair, s_down, s_up, s_relay = slot(), slot(2), slot(2), slot(2)
    f_right, f_left, f_opp = slot(2), slot(2), slot(2)
    push(cells_of(g, far_q), s_down, left, own(far_q))
    push(cells_of(g, 2 + far_q), s_up, right, own(2 + far_q))
    push(d_ref.at[g], s_pair, pair, s_ref)
    push(cells_of(g, mine_q), s_down + 1, left, own(mine_q))
    push(cells_of(g, 2 + mine_q), s_up + 1, right, own(2 + mine_q))

    def split_into(block, first, n):
        where = lanes(first, n)
        hi_ref[block, :, where], lo_ref[block, :, where] = split2(d_ref[block, :, where])

    def product(a, b, segments, first=0, rows=ROWS):
        total = None
        for begin, n in segments:
            where = lanes(begin, n)
            a_hi, a_lo = hi_ref[a, pl.ds(first, rows), where], lo_ref[a, pl.ds(first, rows), where]
            b_hi, b_lo = hi_ref[b, :, where], lo_ref[b, :, where]
            both = dot_nt(jnp.concatenate([a_hi, a_lo], axis=0), b_hi)
            term = both[:rows] + (both[rows:] + dot_nt(a_hi, b_lo))
            total = term if total is None else total + term
        return total * (1.0 / cells)

    def put(kind, position, block):
        rows = block.shape[0] // NX
        for k in range(NX):
            parts[k, kind, pl.ds(position, rows // 8)] = block[rows * k:rows * (k + 1)].reshape(rows // 8, 8, 128)

    class Sums:
        def __init__(self, lo, n):
            self.kinds = pl.ds(lo, n)
            self.x, self.z, self.y = slot(NX), slot(NZ), slot(NY)

        def send_x(self):
            for k in (2, 1, 3):
                push(xin.at[k - 1, self.kinds], self.x + k, x_peer(k), parts.at[(x + k) % NX, self.kinds])

        def send_z(self):
            total = parts[x, self.kinds]
            for k in range(1, NX):
                arrived(xin.at[k - 1, self.kinds], self.x + k)
                total += xin[k - 1, self.kinds]
            xsum[self.kinds] = total
            for k in RING_ORDER:
                push(zin.at[k - 1, self.kinds], self.z + k, z_peer(k), xsum.at[self.kinds, (z + k) % NZ])

        def send_y(self):
            total = xsum[self.kinds, z]
            for k in range(1, NZ):
                arrived(zin.at[k - 1, self.kinds], self.z + k)
                total += zin[k - 1, self.kinds]
            ysum[y, self.kinds] = total
            for k in RING_ORDER:
                push(ysum.at[y, self.kinds], self.y + k, y_peer(y + k))

        def finish(self):
            for k in range(1, NY):
                arrived(ysum.at[(y + NY - k) % NY, self.kinds], self.y + k)

    class Spread:
        def __init__(self, lo, n):
            self.tiles = pl.ds(lo, n)
            self.z, self.x, self.pair = slot(NZ), slot(NX), slot(NX)

        def part(self, core2, k):
            return f_ref.at[core2, (x + NX - k) % NX, :, self.tiles]

        def send_z(self):
            for k in RING_ORDER:
                push(f_ref.at[core, x, z, self.tiles], self.z + k, z_peer(k))

        def send_x(self):
            for k in range(1, NZ):
                arrived(f_ref.at[core, x, (z + NZ - k) % NZ, self.tiles], self.z + k)
            for k in (2, 1, 3):
                push(self.part(core, 0), self.x + k, x_peer(k))
            push(self.part(core, 0), self.pair, pair)

        def send_pair(self):
            for k in (1, 3, 2):
                arrived(self.part(core, k), self.x + k)
                push(self.part(core, k), self.pair + k, pair)

        def finish(self):
            for k in range(NX):
                arrived(self.part(1 - core, k), self.pair + k)

    sum_own, sum_near, sum_opp = Sums(0, 1), Sums(1, 2), Sums(3, 1)
    all_own, all_near, all_opp = Spread(0, NYH), Spread(NYH, NYH), Spread(2 * NYH, 2)

    mine.wait()
    split_into(g, 0, 4)
    put(0, 0, product(g, g, [(0, 4)]))
    arrived(d_ref.at[p_own], s_pair)
    split_into(p_own, 0, 4)
    halfrows = ROWS // 2
    first = pl.multiple_of(halfrows * core, halfrows)
    put(0, 4, product(gx_at(yh, 0), gx_at(yh, 1), [(0, 4)], first, halfrows))
    for k in range(NX):
        parts[k, 0, 6:8] = jnp.zeros((2, 8, 128), f32)
    sum_own.send_x()

    arrived(cells_of(g_right, right_q), s_down)
    push(cells_of(g_right, right_q), s_relay, left)
    push(cells_of(g_right, right_q), f_right, pair)
    arrived(cells_of(g_left, 2 + left_q), s_up)
    push(cells_of(g_left, 2 + left_q), s_relay + 1, right)
    push(cells_of(g_left, 2 + left_q), f_left, pair)
    sum_own.send_z()
    arrived(cells_of(g_right, 1 - right_q), s_down + 1)
    push(cells_of(g_right, 1 - right_q), f_right + 1, pair)
    arrived(cells_of(g_left, 3 - left_q), s_up + 1)
    push(cells_of(g_left, 3 - left_q), f_left + 1, pair)
    l_right, l_left, l_relay, l_pair = slot(), slot(), slot(2), slot(4)
    push(cells_of(g_right, 1 - right_q), l_relay, left)
    push(cells_of(g_left, 3 - left_q), l_relay + 1, right)
    push(cells_of(g, 0, 2), l_right, right, own(0, 2))
    push(cells_of(g, 2, 2), l_left, left, own(2, 2))
    sum_own.send_y()
    split_into(g_right, 0, 2)
    split_into(g_left, 2, 2)
    for c in range(2):
        put(2, 4 * c, product(g_left, gx_at(yh, c), [(2, 2)]))
    put(1, 4 * core, product(g, g_right, [(0, 2)]))
    arrived(cells_of(p_right, right_q), f_right)
    arrived(cells_of(p_right, 1 - right_q), f_right + 1)
    split_into(p_right, 0, 2)
    put(1, 4 * (1 - core), product(g, p_right, [(0, 2)]))
    sum_near.send_x()
    sum_own.finish()
    for k in range(NYH):
        f_ref[core, x, z, k] = ysum[2 * k, 0] + ysum[2 * k + 1, 0]
    all_own.send_z()

    arrived(cells_of(g_opp, mine_q), s_relay)
    push(cells_of(g_opp, mine_q), f_opp, pair)
    arrived(cells_of(g_opp, 2 + mine_q), s_relay + 1)
    push(cells_of(g_opp, 2 + mine_q), f_opp + 1, pair)
    split_into(g_opp, mine_q, 1)
    split_into(g_opp, 2 + mine_q, 1)
    sum_near.send_z()
    segments = [(mine_q, 1), (2 + mine_q, 1)]
    put(3, 4 * core, product(gx_at(yh % 2, core), gx_at(yh % 2 + 2, core), segments))
    arrived(cells_of(p_opp, mine_q), f_opp)
    split_into(p_opp, mine_q, 1)
    arrived(cells_of(p_opp, 2 + mine_q), f_opp + 1)
    split_into(p_opp, 2 + mine_q, 1)
    put(3, 4 * (1 - core), product(gx_at(yh % 2, core), gx_at(yh % 2 + 2, 1 - core), segments))
    sum_opp.send_x()
    all_own.send_x()
    sum_near.send_y()
    sum_opp.send_z()
    sum_near.finish()
    for k in range(NYH):
        after = (k + 1) % NYH
        f_ref[core, x, z, NYH + k] = (ysum[2 * k, 1] + ysum[2 * k + 1, 1]) + (ysum[2 * after, 2] + ysum[2 * after + 1, 2])
    all_near.send_z()
    sum_opp.send_y()
    all_own.send_pair()
    sum_opp.finish()
    for k in range(2):
        f_ref[core, x, z, 2 * NYH + k] = (ysum[2 * k, 3] + ysum[2 * k + 1, 3]) + (ysum[2 * k + 4, 3] + ysum[2 * k + 5, 3])
    all_opp.send_z()
    all_near.send_x()
    arrived(cells_of(g_opp, far_q), l_relay)
    push(cells_of(g_opp, far_q), l_pair, pair)
    arrived(cells_of(g_opp, 2 + far_q), l_relay + 1)
    push(cells_of(g_opp, 2 + far_q), l_pair + 1, pair)
    arrived(cells_of(g_left, 0, 2), l_right)
    push(cells_of(g_left, 0, 2), l_pair + 2, pair)
    arrived(cells_of(g_right, 2, 2), l_left)
    push(cells_of(g_right, 2, 2), l_pair + 3, pair)
    split_into(g_opp, far_q, 1)
    split_into(g_opp, 2 + far_q, 1)
    all_opp.send_x()
    split_into(g_left, 0, 2)
    split_into(g_right, 2, 2)
    arrived(cells_of(p_left, 2 + left_q), f_left)
    arrived(cells_of(p_left, 3 - left_q), f_left + 1)
    split_into(p_left, 2, 2)
    all_near.send_pair()
    arrived(cells_of(p_opp, far_q), l_pair)
    split_into(p_opp, far_q, 1)
    arrived(cells_of(p_opp, 2 + far_q), l_pair + 1)
    split_into(p_opp, 2 + far_q, 1)
    all_opp.send_pair()
    arrived(cells_of(p_left, 0, 2), l_pair + 2)
    split_into(p_left, 0, 2)
    arrived(cells_of(p_right, 2, 2), l_pair + 3)
    split_into(p_right, 2, 2)
    for group in (all_own, all_near, all_opp):
        group.finish()
    for op in sent:
        op.wait_send()


TILES = 2 * NYH + 2
SLOTS = 13 + 8 + 3 * (NX + NZ + NY) + 3 * (NZ + 2 * NX)


def gather_and_gram(snapshot, all_cells):
    cols = snapshot.shape[1]
    vmem = pl.BlockSpec(memory_space=pltpu.VMEM)
    return pl.pallas_call(
        functools.partial(gram_kernel, all_cells),
        out_shape=(jax.ShapeDtypeStruct((G, ROWS, cols), bf16),
                   jax.ShapeDtypeStruct((G, ROWS, cols), bf16),
                   jax.ShapeDtypeStruct((2, NX, NZ, TILES, 8, 128), f32)),
        in_specs=[vmem],
        out_specs=(vmem, vmem, vmem),
        scratch_shapes=[
            pltpu.VMEM((G, ROWS, cols), f32),
            pltpu.VMEM((NX, KINDS, NZ, 8, 128), f32),
            pltpu.VMEM((NX - 1, KINDS, NZ, 8, 128), f32),
            pltpu.VMEM((KINDS, NZ, 8, 128), f32),
            pltpu.VMEM((NZ - 1, KINDS, 8, 128), f32),
            pltpu.VMEM((NY, KINDS, 8, 128), f32),
            pltpu.SemaphoreType.DMA((SLOTS,)),
            pltpu.SemaphoreType.DMA((SLOTS,)),
            pltpu.SemaphoreType.DMA,
        ],
        compiler_params=pltpu.CompilerParams(
            collective_id=0, has_side_effects=True, vmem_limit_bytes=28 * 2**20),
    )(snapshot)


def dot(a, b):
    return lax.dot_general(a, b, (((1,), (0,)), ((), ())), preferred_element_type=f32)


def dot3(a, b_hi, b_lo, nt=False):
    d = dot_nt if nt else dot
    m = a.shape[0]
    a_hi, a_lo = split2(a)
    both = d(jnp.concatenate([a_hi, a_lo], axis=0), b_hi)
    return both[:m] + (both[m:] + d(a_hi, b_lo))


def reciprocal(x):
    r = pl.reciprocal(x, approx=True)
    return r * (2.0 - x * r)


def inverse_factor(m, w_ref):
    n = RANK
    lane = lax.broadcasted_iota(jnp.int32, (8, 128), 1)
    row = lax.broadcasted_iota(jnp.int32, (8, 128), 0)
    js = range(8)
    full = lambda v: jnp.broadcast_to(v, (8, 128))

    def stack(rows):
        t = rows[0]
        for j in js[1:]:
            t = jnp.where(row == j, rows[j], t)
        return t

    rest = jnp.concatenate([m, jnp.zeros((n, 256 - n), f32)], axis=1)
    for p0 in range(0, n, PANEL):
        tiles = [[rest[8 * i:8 * i + 8, 128 * h:128 * h + 128] for h in range(2)] for i in range(PANEL // 8)]
        below = rest[PANEL:]
        ct = p0 // 128
        for gi in range(PANEL // 8):
            c0 = p0 + 8 * gi
            cl = c0 - 128 * ct
            here = (lane >= cl) & (lane < cl + 8)
            t = tiles[gi]
            piv = [[None] * 8 for _ in js]
            for j in js:
                col = full(t[ct][:, cl + j:cl + j + 1])
                for i in range(j + 1):
                    piv[i][j] = full(col[i:i + 1])
            r = [[full(t[h][j:j + 1]) for h in range(2)] for j in js]
            for j in js:
                r[j][ct] = jnp.where(here, jnp.where(lane == cl + j, 1.0, 0.0), r[j][ct])
            inv = [None] * 8
            for j in js:
                inv[j] = reciprocal(piv[j][j])
                for i in range(j + 1, 8):
                    l = piv[j][i] * inv[j]
                    for k in range(i, 8):
                        piv[i][k] = piv[i][k] - l * piv[j][k]
                    for h in range(2):
                        r[i][h] = r[i][h] - l * r[j][h]
            for h in range(2):
                w = stack([r[j][h] * lax.rsqrt(piv[j][j]) for j in js])
                w_ref[c0:c0 + 8, 128 * h:128 * h + 128] = jnp.where(lane + 128 * h <= row + c0, w, 0.0)
            z = [None] * 8
            for j in reversed(js):
                z[j] = []
                for h in range(2):
                    v = r[j][h]
                    for i in range(7, j, -1):
                        v = v - piv[j][i] * z[i][h]
                    z[j].append(v * inv[j])
            for i in range(PANEL // 8):
                if i == gi:
                    continue
                cols = [full(tiles[i][ct][:, cl + j:cl + j + 1]) for j in js]
                old = tiles[i]
                tiles[i] = []
                for h in range(2):
                    v = jnp.where(here, 0.0, old[h]) if h == ct else old[h]
                    even = sum(cols[j] * z[j][h] for j in js[0::2])
                    odd = sum(cols[j] * z[j][h] for j in js[1::2])
                    tiles[i].append(v - (even + odd))
            tiles[gi] = [stack([z[j][h] for j in js]) for h in range(2)]
        if p0 + PANEL < n:
            a = jnp.concatenate([jnp.concatenate(t, axis=1) for t in tiles], axis=0)
            parts = [a]
            if p0 > 128 * ct:
                parts = [jnp.zeros((p0 - 128 * ct, 256), f32)] + parts
            after = 128 * ct + 128 - p0 - PANEL
            if after:
                parts = parts + [jnp.zeros((after, 256), f32)]
            z_hi, z_lo = split2(jnp.concatenate(parts, axis=0))
            lanes = lax.broadcasted_iota(jnp.int32, (1, 256), 1)
            in_panel = (lanes >= p0) & (lanes < p0 + PANEL)
            cut = [below[:PANEL], below[PANEL:]] if below.shape[0] > PANEL else [below]
            rest = jnp.concatenate([
                jnp.where(in_panel, 0.0, v) - dot3(v[:, 128 * ct:128 * ct + 128], z_hi, z_lo) for v in cut], axis=0)


def iterate_kernel(hi_ref, lo_ref, f_ref, start_ref, basis_ref, out_ref, g_hi, g_lo, i_ref, w_ref):
    g = lax.axis_index("gx")


    def store(i, j, block):
        hi, lo = split2(block)
        g_hi[ROWS * i:ROWS * (i + 1), ROWS * j:ROWS * (j + 1)] = hi
        g_lo[ROWS * i:ROWS * (i + 1), ROWS * j:ROWS * (j + 1)] = lo

    def rows(core, tile, first, count):
        own = [f_ref[core, k, :, tile].reshape(NZ * 8, 128)[first:first + count] for k in range(NX)]
        return jnp.concatenate(own, axis=0)

    for yh in range(NYH):
        a, b = 2 * yh, 2 * yh + 1
        pair = jnp.concatenate([rows(0, yh, 32, 16), rows(1, yh, 32, 16)], axis=0)
        store(a, b, pair)
        store(b, a, pair.T)
        for core in range(2):
            i = 2 * yh + core
            store(i, i, rows(core, yh, 0, 32))
            for c in range(2):
                j = 2 * ((yh + 1) % NYH) + c
                block = rows(core, NYH + yh, 32 * c, 32)
                store(i, j, block)
                store(j, i, block.T)
                if yh < 2:
                    j = 2 * (yh + 2) + c
                    block = rows(core, 2 * NYH + yh, 32 * c, 32)
                    store(i, j, block)
                    store(j, i, block.T)

    i_ref[...] = dot3(start_ref[...], g_hi[...], g_lo[...])

    def factor(i_hi, i_lo):
        both = dot_nt(jnp.concatenate([i_hi, i_lo], axis=0), i_hi)
        inverse_factor(both[:RANK] + (both[RANK:] + dot_nt(i_hi, i_lo)), w_ref)

    def times(i_hi, i_lo, b_hi, b_lo):
        both = dot(jnp.concatenate([i_hi, i_lo], axis=0), b_hi)
        return both[:RANK] + (both[RANK:] + dot(i_hi, b_lo))

    def step(_, carry):
        i_hi, i_lo = split2(i_ref[...])
        after = times(i_hi, i_lo, g_hi[...], g_lo[...])
        factor(i_hi, i_lo)
        i_ref[...] = dot3(w_ref[:, :RANK], *split2(after))
        return carry

    lax.fori_loop(0, ITERS - 1, step, 0)
    i_hi, i_lo = split2(i_ref[...])
    after = times(i_hi, i_lo, hi_ref[...], lo_ref[...])
    factor(i_hi, i_lo)
    w = w_ref[:, :RANK]
    core = dot3(w, *split2(after))
    mine_t = dot3(w, *split2(i_ref[:, pl.ds(pl.multiple_of(g * ROWS, ROWS), ROWS)]))
    basis_ref[...] = mine_t
    out_ref[...] = dot3(mine_t.T, *split2(core))


def iterate(d_hi, d_lo, sums, start_t):
    cols = d_hi.shape[1]
    vmem = pl.BlockSpec(memory_space=pltpu.VMEM)
    return pl.pallas_call(
        iterate_kernel,
        out_shape=(jax.ShapeDtypeStruct((RANK, ROWS), f32), jax.ShapeDtypeStruct((ROWS, cols), f32)),
        in_specs=[vmem] * 4,
        out_specs=(vmem, vmem),
        scratch_shapes=[
            pltpu.VMEM((N, N), bf16), pltpu.VMEM((N, N), bf16),
            pltpu.VMEM((RANK, N), f32), pltpu.VMEM((RANK, 256), f32)],
        compiler_params=pltpu.CompilerParams(vmem_limit_bytes=28 * 2**20),
    )(d_hi, d_lo, sums, start_t)


def body(snapshot, start):
    all_cells = snapshot.shape[1] * lax.axis_size("yz")
    d_hi, d_lo, sums = gather_and_gram(snapshot, all_cells)
    shape = (N, snapshot.shape[1])
    basis_t, projected = iterate(d_hi.reshape(shape), d_lo.reshape(shape), sums, start.T)
    return basis_t.T, projected


def solution(mesh):
    in_specs = (P("gx", "yz"), P())
    out_specs = (P("gx", None), P("gx", "yz"))
    return jax.shard_map(body, mesh=mesh, in_specs=in_specs, out_specs=out_specs, check_vma=False)
```

```python
import functools
import jax
import jax.numpy as jnp
from jax import lax
from jax.experimental import pallas as pl
from jax.experimental.pallas import tpu as pltpu
from jax.sharding import PartitionSpec as P

ITERS = 4
G, NYH, NZ, NX, NYL, NY = 8, 4, 8, 4, 2, 8
ROWS = 128
KINDS = 4
RING_ORDER = (4, 3, 5, 2, 6, 1, 7)
N = 1024
RANK = 192
PANEL = 32
f32, bf16 = jnp.float32, jnp.bfloat16
MESH = pl.DeviceIdType.MESH


def split2(a):
    hi = a.astype(jnp.bfloat16)
    lo = (a - hi.astype(jnp.float32)).astype(jnp.bfloat16)
    return hi, lo


def dot_nt(a, b):
    return lax.dot_general(a, b, (((1,), (1,)), ((), ())), preferred_element_type=jnp.float32)


def gram_kernel(cells, s_ref, hi_ref, lo_ref, f_ref, rest_right, rest_left, rest_opp, d_ref, parts, xin, xsum, zin, ysum, send, recv, local):
    g = lax.axis_index("gx")
    q = lax.axis_index("yz")
    yh, core = g // 2, g % 2
    z, x, yl = q // (NX * NYL), (q // NYL) % NX, q % NYL
    y = yh * NYL + yl

    def gx_at(yh2, core2):
        return (yh2 % NYH) * 2 + core2

    def yz_at(z2, x2, yl2):
        return ((z2 % NZ) * NX + x2 % NX) * NYL + yl2

    def y_peer(y2):
        return (gx_at((y2 % NY) // NYL, core), yz_at(z, x, y2 % NYL))

    def x_peer(k):
        return (g, yz_at(z, x + k, yl))

    def z_peer(k):
        return (g, yz_at(z + k, x, yl))

    pair = (gx_at(yh, 1 - core), q)
    right, left = (gx_at(yh + 1, core), q), (gx_at(yh + 3, core), q)
    peers = [pair] + [y_peer(y + k) for k in range(1, NY)]
    peers += [x_peer(k) for k in range(1, NX)] + [z_peer(k) for k in range(1, NZ)]

    barrier = pltpu.get_barrier_semaphore()
    for peer in peers:
        pl.semaphore_signal(barrier, inc=1, device_id=peer, device_id_type=MESH)
    mine = pltpu.make_async_copy(s_ref, d_ref.at[g], local)
    mine.start()
    pl.semaphore_wait(barrier, len(peers))

    sent = []
    count = [0]

    def slot(n=1):
        count[0] += n
        return count[0] - n

    def copy(src, dst, index, target):
        return pltpu.make_async_remote_copy(
            src_ref=src, dst_ref=dst, send_sem=send.at[index], recv_sem=recv.at[index],
            device_id=target, device_id_type=MESH)

    def push(ref, index, target, src=None):
        op = copy(ref if src is None else src, ref, index, target)
        op.start()
        sent.append(op)

    def arrived(ref, index):
        copy(ref, ref, index, pair).wait_recv()

    quarter = s_ref.shape[1] // 4
    mine_q = yh // 2
    far_q = 1 - mine_q
    right_q = 1 - (yh + 1) % NYH // 2
    left_q = 1 - (yh + 3) % NYH // 2

    def lanes(first, n):
        return pl.ds(pl.multiple_of(first * quarter, quarter), n * quarter)

    def cells_of(block, first, n=1):
        return d_ref.at[block, :, lanes(first, n)]

    def own(first, n=1):
        return s_ref.at[:, lanes(first, n)]

    g_right, g_left, g_opp = right[0], left[0], gx_at(yh + 2, core)
    p_own = pair[0]
    p_right, p_left, p_opp = (gx_at(yh + k, 1 - core) for k in (1, 3, 2))
    s_pair, s_down, s_up, s_relay = slot(), slot(2), slot(2), slot(2)
    f_right, f_left, f_opp = slot(2), slot(2), slot(2)
    push(cells_of(g, far_q), s_down, left, own(far_q))
    push(cells_of(g, 2 + far_q), s_up, right, own(2 + far_q))
    push(d_ref.at[g], s_pair, pair, s_ref)
    push(cells_of(g, mine_q), s_down + 1, left, own(mine_q))
    push(cells_of(g, 2 + mine_q), s_up + 1, right, own(2 + mine_q))

    def split_into(block, first, n):
        where = lanes(first, n)
        hi_ref[block, :, where], lo_ref[block, :, where] = split2(d_ref[block, :, where])

    def product(a, b, segments, first=0, rows=ROWS):
        total = None
        for begin, n in segments:
            where = lanes(begin, n)
            a_hi, a_lo = hi_ref[a, pl.ds(first, rows), where], lo_ref[a, pl.ds(first, rows), where]
            b_hi, b_lo = hi_ref[b, :, where], lo_ref[b, :, where]
            both = dot_nt(jnp.concatenate([a_hi, a_lo], axis=0), b_hi)
            term = both[:rows] + (both[rows:] + dot_nt(a_hi, b_lo))
            total = term if total is None else total + term
        return total * (1.0 / cells)

    def put(kind, position, block):
        rows = block.shape[0] // NX
        for k in range(NX):
            parts[k, kind, pl.ds(position, rows // 8)] = block[rows * k:rows * (k + 1)].reshape(rows // 8, 8, 128)

    class Sums:
        def __init__(self, lo, n):
            self.kinds = pl.ds(lo, n)
            self.x, self.z, self.y = slot(NX), slot(NZ), slot(NY)

        def send_x(self):
            for k in (2, 1, 3):
                push(xin.at[k - 1, self.kinds], self.x + k, x_peer(k), parts.at[(x + k) % NX, self.kinds])

        def send_z(self):
            total = parts[x, self.kinds]
            for k in range(1, NX):
                arrived(xin.at[k - 1, self.kinds], self.x + k)
                total += xin[k - 1, self.kinds]
            xsum[self.kinds] = total
            for k in RING_ORDER:
                push(zin.at[k - 1, self.kinds], self.z + k, z_peer(k), xsum.at[self.kinds, (z + k) % NZ])

        def send_y(self):
            total = xsum[self.kinds, z]
            for k in range(1, NZ):
                arrived(zin.at[k - 1, self.kinds], self.z + k)
                total += zin[k - 1, self.kinds]
            ysum[y, self.kinds] = total
            for k in RING_ORDER:
                push(ysum.at[y, self.kinds], self.y + k, y_peer(y + k))

        def finish(self):
            for k in range(1, NY):
                arrived(ysum.at[(y + NY - k) % NY, self.kinds], self.y + k)

    class Spread:
        def __init__(self, lo, n):
            self.tiles = pl.ds(lo, n)
            self.z, self.x, self.pair = slot(NZ), slot(NX), slot(NX)

        def part(self, core2, k):
            return f_ref.at[core2, (x + NX - k) % NX, :, self.tiles]

        def send_z(self):
            for k in RING_ORDER:
                push(f_ref.at[core, x, z, self.tiles], self.z + k, z_peer(k))

        def send_x(self):
            for k in range(1, NZ):
                arrived(f_ref.at[core, x, (z + NZ - k) % NZ, self.tiles], self.z + k)
            for k in (2, 1, 3):
                push(self.part(core, 0), self.x + k, x_peer(k))
            push(self.part(core, 0), self.pair, pair)

        def send_pair(self):
            for k in (1, 3, 2):
                arrived(self.part(core, k), self.x + k)
                push(self.part(core, k), self.pair + k, pair)

        def finish(self):
            for k in range(NX):
                arrived(self.part(1 - core, k), self.pair + k)

    sum_own, sum_near, sum_opp = Sums(0, 1), Sums(1, 2), Sums(3, 1)
    all_own, all_near, all_opp = Spread(0, NYH), Spread(NYH, NYH), Spread(2 * NYH, 2)

    mine.wait()
    split_into(g, 0, 4)
    put(0, 0, product(g, g, [(0, 4)]))
    arrived(d_ref.at[p_own], s_pair)
    split_into(p_own, 0, 4)
    halfrows = ROWS // 2
    first = pl.multiple_of(halfrows * core, halfrows)
    put(0, 4, product(gx_at(yh, 0), gx_at(yh, 1), [(0, 4)], first, halfrows))
    for k in range(NX):
        parts[k, 0, 6:8] = jnp.zeros((2, 8, 128), f32)
    sum_own.send_x()
    rest_right[...] = d_ref[g, :, :2 * quarter]
    rest_left[...] = d_ref[g, :, 2 * quarter:]
    rest_opp[:, :quarter] = d_ref[g, :, lanes(mine_q, 1)]
    rest_opp[:, quarter:] = d_ref[g, :, lanes(2 + mine_q, 1)]
    for block, gap in ((g_left, 0), (p_left, 0), (g_right, 2), (p_right, 2)):
        hi_ref[block, :, lanes(gap, 2)] = jnp.zeros((ROWS, 2 * quarter), bf16)
        lo_ref[block, :, lanes(gap, 2)] = jnp.zeros((ROWS, 2 * quarter), bf16)
    for block in (g_opp, p_opp):
        for gap in (far_q, 2 + far_q):
            hi_ref[block, :, lanes(gap, 1)] = jnp.zeros((ROWS, quarter), bf16)
            lo_ref[block, :, lanes(gap, 1)] = jnp.zeros((ROWS, quarter), bf16)

    arrived(cells_of(g_right, right_q), s_down)
    push(cells_of(g_right, right_q), s_relay, left)
    push(cells_of(g_right, right_q), f_right, pair)
    arrived(cells_of(g_left, 2 + left_q), s_up)
    push(cells_of(g_left, 2 + left_q), s_relay + 1, right)
    push(cells_of(g_left, 2 + left_q), f_left, pair)
    sum_own.send_z()
    arrived(cells_of(g_right, 1 - right_q), s_down + 1)
    push(cells_of(g_right, 1 - right_q), f_right + 1, pair)
    arrived(cells_of(g_left, 3 - left_q), s_up + 1)
    push(cells_of(g_left, 3 - left_q), f_left + 1, pair)
    sum_own.send_y()
    split_into(g_right, 0, 2)
    split_into(g_left, 2, 2)
    for c in range(2):
        put(2, 4 * c, product(g_left, gx_at(yh, c), [(2, 2)]))
    put(1, 4 * core, product(g, g_right, [(0, 2)]))
    arrived(cells_of(p_right, right_q), f_right)
    arrived(cells_of(p_right, 1 - right_q), f_right + 1)
    split_into(p_right, 0, 2)
    put(1, 4 * (1 - core), product(g, p_right, [(0, 2)]))
    sum_near.send_x()
    sum_own.finish()
    for k in range(NYH):
        f_ref[core, x, z, k] = ysum[2 * k, 0] + ysum[2 * k + 1, 0]
    all_own.send_z()

    arrived(cells_of(g_opp, mine_q), s_relay)
    push(cells_of(g_opp, mine_q), f_opp, pair)
    arrived(cells_of(g_opp, 2 + mine_q), s_relay + 1)
    push(cells_of(g_opp, 2 + mine_q), f_opp + 1, pair)
    split_into(g_opp, mine_q, 1)
    split_into(g_opp, 2 + mine_q, 1)
    sum_near.send_z()
    segments = [(mine_q, 1), (2 + mine_q, 1)]
    put(3, 4 * core, product(gx_at(yh % 2, core), gx_at(yh % 2 + 2, core), segments))
    arrived(cells_of(p_opp, mine_q), f_opp)
    split_into(p_opp, mine_q, 1)
    arrived(cells_of(p_opp, 2 + mine_q), f_opp + 1)
    split_into(p_opp, 2 + mine_q, 1)
    put(3, 4 * (1 - core), product(gx_at(yh % 2, core), gx_at(yh % 2 + 2, 1 - core), segments))
    sum_opp.send_x()
    all_own.send_x()
    sum_near.send_y()
    sum_opp.send_z()
    sum_near.finish()
    for k in range(NYH):
        after = (k + 1) % NYH
        f_ref[core, x, z, NYH + k] = (ysum[2 * k, 1] + ysum[2 * k + 1, 1]) + (ysum[2 * after, 2] + ysum[2 * after + 1, 2])
    all_near.send_z()
    sum_opp.send_y()
    all_own.send_pair()
    sum_opp.finish()
    for k in range(2):
        f_ref[core, x, z, 2 * NYH + k] = (ysum[2 * k, 3] + ysum[2 * k + 1, 3]) + (ysum[2 * k + 4, 3] + ysum[2 * k + 5, 3])
    all_opp.send_z()
    all_near.send_x()
    all_opp.send_x()
    arrived(cells_of(p_left, 2 + left_q), f_left)
    arrived(cells_of(p_left, 3 - left_q), f_left + 1)
    split_into(p_left, 2, 2)
    all_near.send_pair()
    all_opp.send_pair()
    for group in (all_own, all_near, all_opp):
        group.finish()
    for op in sent:
        op.wait_send()


TILES = 2 * NYH + 2
SLOTS = 13 + 3 * (NX + NZ + NY) + 3 * (NZ + 2 * NX)


def gather_and_gram(snapshot, all_cells):
    cols = snapshot.shape[1]
    vmem = pl.BlockSpec(memory_space=pltpu.VMEM)
    return pl.pallas_call(
        functools.partial(gram_kernel, all_cells),
        out_shape=(jax.ShapeDtypeStruct((G, ROWS, cols), bf16),
                   jax.ShapeDtypeStruct((G, ROWS, cols), bf16),
                   jax.ShapeDtypeStruct((2, NX, NZ, TILES, 8, 128), f32),
                   *[jax.ShapeDtypeStruct((ROWS, cols // 2), f32)] * 3),
        in_specs=[vmem],
        out_specs=(vmem,) * 6,
        scratch_shapes=[
            pltpu.VMEM((G, ROWS, cols), f32),
            pltpu.VMEM((NX, KINDS, NZ, 8, 128), f32),
            pltpu.VMEM((NX - 1, KINDS, NZ, 8, 128), f32),
            pltpu.VMEM((KINDS, NZ, 8, 128), f32),
            pltpu.VMEM((NZ - 1, KINDS, 8, 128), f32),
            pltpu.VMEM((NY, KINDS, 8, 128), f32),
            pltpu.SemaphoreType.DMA((SLOTS,)),
            pltpu.SemaphoreType.DMA((SLOTS,)),
            pltpu.SemaphoreType.DMA,
        ],
        compiler_params=pltpu.CompilerParams(
            collective_id=0, has_side_effects=True, vmem_limit_bytes=28 * 2**20),
    )(snapshot)


def dot(a, b):
    return lax.dot_general(a, b, (((1,), (0,)), ((), ())), preferred_element_type=f32)


def dot3(a, b_hi, b_lo, nt=False):
    d = dot_nt if nt else dot
    m = a.shape[0]
    a_hi, a_lo = split2(a)
    both = d(jnp.concatenate([a_hi, a_lo], axis=0), b_hi)
    return both[:m] + (both[m:] + d(a_hi, b_lo))


def reciprocal(x):
    r = pl.reciprocal(x, approx=True)
    return r * (2.0 - x * r)


def inverse_factor(m, w_ref):
    n = RANK
    lane = lax.broadcasted_iota(jnp.int32, (8, 128), 1)
    row = lax.broadcasted_iota(jnp.int32, (8, 128), 0)
    js = range(8)
    full = lambda v: jnp.broadcast_to(v, (8, 128))

    def stack(rows):
        t = rows[0]
        for j in js[1:]:
            t = jnp.where(row == j, rows[j], t)
        return t

    rest = jnp.concatenate([m, jnp.zeros((n, 256 - n), f32)], axis=1)
    for p0 in range(0, n, PANEL):
        tiles = [[rest[8 * i:8 * i + 8, 128 * h:128 * h + 128] for h in range(2)] for i in range(PANEL // 8)]
        below = rest[PANEL:]
        ct = p0 // 128
        for gi in range(PANEL // 8):
            c0 = p0 + 8 * gi
            cl = c0 - 128 * ct
            here = (lane >= cl) & (lane < cl + 8)
            t = tiles[gi]
            piv = [[None] * 8 for _ in js]
            for j in js:
                col = full(t[ct][:, cl + j:cl + j + 1])
                for i in range(j + 1):
                    piv[i][j] = full(col[i:i + 1])
            r = [[full(t[h][j:j + 1]) for h in range(2)] for j in js]
            for j in js:
                r[j][ct] = jnp.where(here, jnp.where(lane == cl + j, 1.0, 0.0), r[j][ct])
            inv = [None] * 8
            for j in js:
                inv[j] = reciprocal(piv[j][j])
                for i in range(j + 1, 8):
                    l = piv[j][i] * inv[j]
                    for k in range(i, 8):
                        piv[i][k] = piv[i][k] - l * piv[j][k]
                    for h in range(2):
                        r[i][h] = r[i][h] - l * r[j][h]
            for h in range(2):
                w = stack([r[j][h] * lax.rsqrt(piv[j][j]) for j in js])
                w_ref[c0:c0 + 8, 128 * h:128 * h + 128] = jnp.where(lane + 128 * h <= row + c0, w, 0.0)
            z = [None] * 8
            for j in reversed(js):
                z[j] = []
                for h in range(2):
                    v = r[j][h]
                    for i in range(7, j, -1):
                        v = v - piv[j][i] * z[i][h]
                    z[j].append(v * inv[j])
            for i in range(PANEL // 8):
                if i == gi:
                    continue
                cols = [full(tiles[i][ct][:, cl + j:cl + j + 1]) for j in js]
                old = tiles[i]
                tiles[i] = []
                for h in range(2):
                    v = jnp.where(here, 0.0, old[h]) if h == ct else old[h]
                    even = sum(cols[j] * z[j][h] for j in js[0::2])
                    odd = sum(cols[j] * z[j][h] for j in js[1::2])
                    tiles[i].append(v - (even + odd))
            tiles[gi] = [stack([z[j][h] for j in js]) for h in range(2)]
        if p0 + PANEL < n:
            a = jnp.concatenate([jnp.concatenate(t, axis=1) for t in tiles], axis=0)
            parts = [a]
            if p0 > 128 * ct:
                parts = [jnp.zeros((p0 - 128 * ct, 256), f32)] + parts
            after = 128 * ct + 128 - p0 - PANEL
            if after:
                parts = parts + [jnp.zeros((after, 256), f32)]
            z_hi, z_lo = split2(jnp.concatenate(parts, axis=0))
            lanes = lax.broadcasted_iota(jnp.int32, (1, 256), 1)
            in_panel = (lanes >= p0) & (lanes < p0 + PANEL)
            cut = [below[:PANEL], below[PANEL:]] if below.shape[0] > PANEL else [below]
            rest = jnp.concatenate([
                jnp.where(in_panel, 0.0, v) - dot3(v[:, 128 * ct:128 * ct + 128], z_hi, z_lo) for v in cut], axis=0)


def iterate_kernel(hi_ref, lo_ref, f_ref, start_ref, basis_ref, core_ref, g_hi, g_lo, i_ref, w_ref):


    def store(i, j, block):
        hi, lo = split2(block)
        g_hi[ROWS * i:ROWS * (i + 1), ROWS * j:ROWS * (j + 1)] = hi
        g_lo[ROWS * i:ROWS * (i + 1), ROWS * j:ROWS * (j + 1)] = lo

    def rows(core, tile, first, count):
        own = [f_ref[core, k, :, tile].reshape(NZ * 8, 128)[first:first + count] for k in range(NX)]
        return jnp.concatenate(own, axis=0)

    for yh in range(NYH):
        a, b = 2 * yh, 2 * yh + 1
        pair = jnp.concatenate([rows(0, yh, 32, 16), rows(1, yh, 32, 16)], axis=0)
        store(a, b, pair)
        store(b, a, pair.T)
        for core in range(2):
            i = 2 * yh + core
            store(i, i, rows(core, yh, 0, 32))
            for c in range(2):
                j = 2 * ((yh + 1) % NYH) + c
                block = rows(core, NYH + yh, 32 * c, 32)
                store(i, j, block)
                store(j, i, block.T)
                if yh < 2:
                    j = 2 * (yh + 2) + c
                    block = rows(core, 2 * NYH + yh, 32 * c, 32)
                    store(i, j, block)
                    store(j, i, block.T)

    i_ref[...] = dot3(start_ref[...], g_hi[...], g_lo[...])

    def factor(i_hi, i_lo):
        both = dot_nt(jnp.concatenate([i_hi, i_lo], axis=0), i_hi)
        inverse_factor(both[:RANK] + (both[RANK:] + dot_nt(i_hi, i_lo)), w_ref)

    def times(i_hi, i_lo, b_hi, b_lo):
        both = dot(jnp.concatenate([i_hi, i_lo], axis=0), b_hi)
        return both[:RANK] + (both[RANK:] + dot(i_hi, b_lo))

    def step(_, carry):
        i_hi, i_lo = split2(i_ref[...])
        after = times(i_hi, i_lo, g_hi[...], g_lo[...])
        factor(i_hi, i_lo)
        i_ref[...] = dot3(w_ref[:, :RANK], *split2(after))
        return carry

    lax.fori_loop(0, ITERS - 1, step, 0)
    i_hi, i_lo = split2(i_ref[...])
    after = times(i_hi, i_lo, hi_ref[...], lo_ref[...])
    factor(i_hi, i_lo)
    w = w_ref[:, :RANK]
    core_ref[...] = dot3(w, *split2(after))
    basis_ref[...] = dot3(w, i_hi, i_lo)


def project_kernel(basis_ref, core_ref, *refs):
    near_refs, other_refs, (mine_ref, out_ref) = refs[:3], refs[3:6], refs[6:]
    g = lax.axis_index("gx")
    yh, c = g // 2, g % 2
    half = near_refs[0].shape[1]

    def term(k, ahead):
        def of(ref, core):
            block = (yh + ahead) % NYH * 2 + core
            q = basis_ref[:, pl.ds(pl.multiple_of(block * ROWS, ROWS), ROWS)]
            return dot3(q, *split2(ref[...]))
        return of(near_refs[k], c) + of(other_refs[k], 1 - c)

    left, right, opposite = term(0, 3), term(1, 1), term(2, 2)
    far = 1 - yh // 2
    quarter = half // 2
    none = jnp.zeros((RANK, quarter), f32)
    at_second = far == 1

    def placed(piece):
        first = jnp.concatenate([piece, none], axis=1)
        second = jnp.concatenate([none, piece], axis=1)
        return jnp.where(at_second, second, first)

    low = core_ref[:, :half] + left + placed(opposite[:, :quarter])
    high = core_ref[:, half:] + right + placed(opposite[:, quarter:])
    mine_t = basis_ref[:, pl.ds(pl.multiple_of(g * ROWS, ROWS), ROWS)]
    mine_ref[...] = mine_t
    mine = mine_t.T
    out_ref[:, :half] = dot3(mine, *split2(low))
    out_ref[:, half:] = dot3(mine, *split2(high))


def project(basis_t, core, near, other):
    vmem = pl.BlockSpec(memory_space=pltpu.VMEM)
    return pl.pallas_call(
        project_kernel,
        out_shape=(jax.ShapeDtypeStruct((RANK, ROWS), f32), jax.ShapeDtypeStruct((ROWS, core.shape[1]), f32)),
        in_specs=[vmem] * 8,
        out_specs=(vmem, vmem),
        compiler_params=pltpu.CompilerParams(vmem_limit_bytes=16 * 2**20),
    )(basis_t, core, *near, *other)


def iterate(d_hi, d_lo, sums, start_t):
    cols = d_hi.shape[1]
    vmem = pl.BlockSpec(memory_space=pltpu.VMEM)
    return pl.pallas_call(
        iterate_kernel,
        out_shape=(jax.ShapeDtypeStruct((RANK, N), f32), jax.ShapeDtypeStruct((RANK, cols), f32)),
        in_specs=[vmem] * 4,
        out_specs=(vmem, vmem),
        scratch_shapes=[
            pltpu.VMEM((N, N), bf16), pltpu.VMEM((N, N), bf16),
            pltpu.VMEM((RANK, N), f32), pltpu.VMEM((RANK, 256), f32)],
        compiler_params=pltpu.CompilerParams(vmem_limit_bytes=28 * 2**20),
        cost_estimate=pl.CostEstimate(flops=40_000_000_000, bytes_accessed=120_000_000, transcendentals=0),
    )(d_hi, d_lo, sums, start_t)


def body(snapshot, start):
    all_cells = snapshot.shape[1] * lax.axis_size("yz")
    d_hi, d_lo, sums, *rest = gather_and_gram(snapshot, all_cells)
    near = [lax.ppermute(r, "gx", [(i, (i + step) % G) for i in range(G)])
            for r, step in zip(rest, (2, G - 2, G // 2))]
    shape = (N, snapshot.shape[1])
    basis_t, core = iterate(d_hi.reshape(shape), d_lo.reshape(shape), sums, start.T)
    basis_t, core, *near = lax.optimization_barrier((basis_t, core, *near))
    other = [lax.ppermute(r, "gx", [(i, i ^ 1) for i in range(G)]) for r in near]
    mine_t, projected = project(basis_t, core, near, other)
    return mine_t.T, projected


def solution(mesh):
    in_specs = (P("gx", "yz"), P())
    out_specs = (P("gx", None), P("gx", "yz"))
    return jax.shard_map(body, mesh=mesh, in_specs=in_specs, out_specs=out_specs, check_vma=False)
```

```python
import functools
import jax
import jax.numpy as jnp
from jax import lax
from jax.experimental import pallas as pl
from jax.experimental.pallas import tpu as pltpu
from jax.sharding import PartitionSpec as P

ITERS = 4
G, NYH, NZ, NX, NYL, NY = 8, 4, 8, 4, 2, 8
ROWS = 128
KINDS = 4
RING_ORDER = (4, 3, 5, 2, 6, 1, 7)
N = 1024
RANK = 192
PANEL = 32
f32, bf16 = jnp.float32, jnp.bfloat16
MESH = pl.DeviceIdType.MESH


def split2(a):
    hi = a.astype(jnp.bfloat16)
    lo = (a - hi.astype(jnp.float32)).astype(jnp.bfloat16)
    return hi, lo


def dot_nt(a, b):
    return lax.dot_general(a, b, (((1,), (1,)), ((), ())), preferred_element_type=jnp.float32)


def gram_kernel(cells, s_ref, hi_ref, lo_ref, f_ref, d_ref, parts, xin, xsum, zin, ysum, send, recv, local):
    g = lax.axis_index("gx")
    q = lax.axis_index("yz")
    yh, core = g // 2, g % 2
    z, x, yl = q // (NX * NYL), (q // NYL) % NX, q % NYL
    y = yh * NYL + yl

    def gx_at(yh2, core2):
        return (yh2 % NYH) * 2 + core2

    def yz_at(z2, x2, yl2):
        return ((z2 % NZ) * NX + x2 % NX) * NYL + yl2

    def y_peer(y2):
        return (gx_at((y2 % NY) // NYL, core), yz_at(z, x, y2 % NYL))

    def x_peer(k):
        return (g, yz_at(z, x + k, yl))

    def z_peer(k):
        return (g, yz_at(z + k, x, yl))

    pair = (gx_at(yh, 1 - core), q)
    right, left = (gx_at(yh + 1, core), q), (gx_at(yh + 3, core), q)
    peers = [pair] + [y_peer(y + k) for k in range(1, NY)]
    peers += [x_peer(k) for k in range(1, NX)] + [z_peer(k) for k in range(1, NZ)]

    barrier = pltpu.get_barrier_semaphore()
    for peer in peers:
        pl.semaphore_signal(barrier, inc=1, device_id=peer, device_id_type=MESH)
    mine = pltpu.make_async_copy(s_ref, d_ref.at[g], local)
    mine.start()
    pl.semaphore_wait(barrier, len(peers))

    sent = []
    count = [0]

    def slot(n=1):
        count[0] += n
        return count[0] - n

    def copy(src, dst, index, target):
        return pltpu.make_async_remote_copy(
            src_ref=src, dst_ref=dst, send_sem=send.at[index], recv_sem=recv.at[index],
            device_id=target, device_id_type=MESH)

    def push(ref, index, target, src=None):
        op = copy(ref if src is None else src, ref, index, target)
        op.start()
        sent.append(op)

    def arrived(ref, index):
        copy(ref, ref, index, pair).wait_recv()

    quarter = s_ref.shape[1] // 4
    mine_q = yh // 2
    far_q = 1 - mine_q
    right_q = 1 - (yh + 1) % NYH // 2
    left_q = 1 - (yh + 3) % NYH // 2

    def lanes(first, n):
        return pl.ds(pl.multiple_of(first * quarter, quarter), n * quarter)

    def cells_of(block, first, n=1):
        return d_ref.at[block, :, lanes(first, n)]

    def own(first, n=1):
        return s_ref.at[:, lanes(first, n)]

    g_right, g_left, g_opp = right[0], left[0], gx_at(yh + 2, core)
    p_own = pair[0]
    p_right, p_left, p_opp = (gx_at(yh + k, 1 - core) for k in (1, 3, 2))
    s_pair, s_down, s_up, s_relay = slot(), slot(2), slot(2), slot(2)
    f_right, f_left, f_opp = slot(2), slot(2), slot(2)
    push(cells_of(g, far_q), s_down, left, own(far_q))
    push(cells_of(g, 2 + far_q), s_up, right, own(2 + far_q))
    push(d_ref.at[g], s_pair, pair, s_ref)
    push(cells_of(g, mine_q), s_down + 1, left, own(mine_q))
    push(cells_of(g, 2 + mine_q), s_up + 1, right, own(2 + mine_q))

    def split_into(block, first, n):
        where = lanes(first, n)
        hi_ref[block, :, where], lo_ref[block, :, where] = split2(d_ref[block, :, where])

    def product(a, b, segments, first=0, rows=ROWS):
        total = None
        for begin, n in segments:
            where = lanes(begin, n)
            a_hi, a_lo = hi_ref[a, pl.ds(first, rows), where], lo_ref[a, pl.ds(first, rows), where]
            b_hi, b_lo = hi_ref[b, :, where], lo_ref[b, :, where]
            both = dot_nt(jnp.concatenate([a_hi, a_lo], axis=0), b_hi)
            term = both[:rows] + (both[rows:] + dot_nt(a_hi, b_lo))
            total = term if total is None else total + term
        return total * (1.0 / cells)

    def put(kind, position, block):
        rows = block.shape[0] // NX
        for k in range(NX):
            parts[k, kind, pl.ds(position, rows // 8)] = block[rows * k:rows * (k + 1)].reshape(rows // 8, 8, 128)

    class Sums:
        def __init__(self, lo, n):
            self.kinds = pl.ds(lo, n)
            self.x, self.z, self.y = slot(NX), slot(NZ), slot(NY)

        def send_x(self):
            for k in (2, 1, 3):
                push(xin.at[k - 1, self.kinds], self.x + k, x_peer(k), parts.at[(x + k) % NX, self.kinds])

        def send_z(self):
            total = parts[x, self.kinds]
            for k in range(1, NX):
                arrived(xin.at[k - 1, self.kinds], self.x + k)
                total += xin[k - 1, self.kinds]
            xsum[self.kinds] = total
            for k in RING_ORDER:
                push(zin.at[k - 1, self.kinds], self.z + k, z_peer(k), xsum.at[self.kinds, (z + k) % NZ])

        def send_y(self):
            total = xsum[self.kinds, z]
            for k in range(1, NZ):
                arrived(zin.at[k - 1, self.kinds], self.z + k)
                total += zin[k - 1, self.kinds]
            ysum[y, self.kinds] = total
            for k in RING_ORDER:
                push(ysum.at[y, self.kinds], self.y + k, y_peer(y + k))

        def finish(self):
            for k in range(1, NY):
                arrived(ysum.at[(y + NY - k) % NY, self.kinds], self.y + k)

    class Spread:
        def __init__(self, lo, n):
            self.tiles = pl.ds(lo, n)
            self.z, self.x, self.pair = slot(NZ), slot(NX), slot(NX)

        def part(self, core2, k):
            return f_ref.at[core2, (x + NX - k) % NX, :, self.tiles]

        def send_z(self):
            for k in RING_ORDER:
                push(f_ref.at[core, x, z, self.tiles], self.z + k, z_peer(k))

        def send_x(self):
            for k in range(1, NZ):
                arrived(f_ref.at[core, x, (z + NZ - k) % NZ, self.tiles], self.z + k)
            for k in (2, 1, 3):
                push(self.part(core, 0), self.x + k, x_peer(k))
            push(self.part(core, 0), self.pair, pair)

        def send_pair(self):
            for k in (1, 3, 2):
                arrived(self.part(core, k), self.x + k)
                push(self.part(core, k), self.pair + k, pair)

        def finish(self):
            for k in range(NX):
                arrived(self.part(1 - core, k), self.pair + k)

    sum_own, sum_near, sum_opp = Sums(0, 1), Sums(1, 2), Sums(3, 1)
    all_own, all_near, all_opp = Spread(0, NYH), Spread(NYH, NYH), Spread(2 * NYH, 2)

    mine.wait()
    split_into(g, 0, 4)
    put(0, 0, product(g, g, [(0, 4)]))
    arrived(d_ref.at[p_own], s_pair)
    split_into(p_own, 0, 4)
    halfrows = ROWS // 2
    first = pl.multiple_of(halfrows * core, halfrows)
    put(0, 4, product(gx_at(yh, 0), gx_at(yh, 1), [(0, 4)], first, halfrows))
    for k in range(NX):
        parts[k, 0, 6:8] = jnp.zeros((2, 8, 128), f32)
    sum_own.send_x()

    arrived(cells_of(g_right, right_q), s_down)
    push(cells_of(g_right, right_q), s_relay, left)
    push(cells_of(g_right, right_q), f_right, pair)
    arrived(cells_of(g_left, 2 + left_q), s_up)
    push(cells_of(g_left, 2 + left_q), s_relay + 1, right)
    push(cells_of(g_left, 2 + left_q), f_left, pair)
    sum_own.send_z()
    arrived(cells_of(g_right, 1 - right_q), s_down + 1)
    push(cells_of(g_right, 1 - right_q), f_right + 1, pair)
    arrived(cells_of(g_left, 3 - left_q), s_up + 1)
    push(cells_of(g_left, 3 - left_q), f_left + 1, pair)
    sum_own.send_y()
    split_into(g_right, 0, 2)
    split_into(g_left, 2, 2)
    for c in range(2):
        put(2, 4 * c, product(g_left, gx_at(yh, c), [(2, 2)]))
    put(1, 4 * core, product(g, g_right, [(0, 2)]))
    arrived(cells_of(p_right, right_q), f_right)
    arrived(cells_of(p_right, 1 - right_q), f_right + 1)
    split_into(p_right, 0, 2)
    put(1, 4 * (1 - core), product(g, p_right, [(0, 2)]))
    sum_near.send_x()
    l_right, l_left, l_relay, l_pair = slot(2), slot(2), slot(2), slot(6)
    push(cells_of(g_right, 1 - right_q), l_relay, left)
    push(cells_of(g_left, 3 - left_q), l_relay + 1, right)
    sum_own.finish()
    for k in range(NYH):
        f_ref[core, x, z, k] = ysum[2 * k, 0] + ysum[2 * k + 1, 0]
    all_own.send_z()

    arrived(cells_of(g_opp, mine_q), s_relay)
    push(cells_of(g_opp, mine_q), f_opp, pair)
    arrived(cells_of(g_opp, 2 + mine_q), s_relay + 1)
    push(cells_of(g_opp, 2 + mine_q), f_opp + 1, pair)
    push(cells_of(g, 0), l_right, right, own(0))
    push(cells_of(g, 2), l_left, left, own(2))
    split_into(g_opp, mine_q, 1)
    split_into(g_opp, 2 + mine_q, 1)
    sum_near.send_z()
    segments = [(mine_q, 1), (2 + mine_q, 1)]
    put(3, 4 * core, product(gx_at(yh % 2, core), gx_at(yh % 2 + 2, core), segments))
    arrived(cells_of(p_opp, mine_q), f_opp)
    split_into(p_opp, mine_q, 1)
    arrived(cells_of(p_opp, 2 + mine_q), f_opp + 1)
    split_into(p_opp, 2 + mine_q, 1)
    put(3, 4 * (1 - core), product(gx_at(yh % 2, core), gx_at(yh % 2 + 2, 1 - core), segments))
    sum_opp.send_x()
    all_own.send_x()
    sum_near.send_y()
    sum_opp.send_z()
    sum_near.finish()
    for k in range(NYH):
        after = (k + 1) % NYH
        f_ref[core, x, z, NYH + k] = (ysum[2 * k, 1] + ysum[2 * k + 1, 1]) + (ysum[2 * after, 2] + ysum[2 * after + 1, 2])
    all_near.send_z()
    sum_opp.send_y()
    push(cells_of(g, 1), l_right + 1, right, own(1))
    push(cells_of(g, 3), l_left + 1, left, own(3))
    all_own.send_pair()
    sum_opp.finish()
    for k in range(2):
        f_ref[core, x, z, 2 * NYH + k] = (ysum[2 * k, 3] + ysum[2 * k + 1, 3]) + (ysum[2 * k + 4, 3] + ysum[2 * k + 5, 3])
    all_opp.send_z()
    all_near.send_x()
    for k in range(2):
        arrived(cells_of(g_opp, 2 * k + far_q), l_relay + k)
        push(cells_of(g_opp, 2 * k + far_q), l_pair + k, pair)
    arrived(cells_of(g_left, 0), l_right)
    push(cells_of(g_left, 0), l_pair + 2, pair)
    arrived(cells_of(g_right, 2), l_left)
    push(cells_of(g_right, 2), l_pair + 3, pair)
    split_into(g_opp, far_q, 1)
    split_into(g_opp, 2 + far_q, 1)
    all_opp.send_x()
    arrived(cells_of(p_left, 2 + left_q), f_left)
    arrived(cells_of(p_left, 3 - left_q), f_left + 1)
    split_into(p_left, 2, 2)
    all_near.send_pair()
    for k in range(2):
        arrived(cells_of(p_opp, 2 * k + far_q), l_pair + k)
        split_into(p_opp, 2 * k + far_q, 1)
    all_opp.send_pair()
    arrived(cells_of(g_left, 1), l_right + 1)
    push(cells_of(g_left, 1), l_pair + 4, pair)
    arrived(cells_of(g_right, 3), l_left + 1)
    push(cells_of(g_right, 3), l_pair + 5, pair)
    split_into(g_left, 0, 2)
    split_into(g_right, 2, 2)
    arrived(cells_of(p_left, 0), l_pair + 2)
    arrived(cells_of(p_left, 1), l_pair + 4)
    split_into(p_left, 0, 2)
    arrived(cells_of(p_right, 2), l_pair + 3)
    arrived(cells_of(p_right, 3), l_pair + 5)
    split_into(p_right, 2, 2)
    for group in (all_own, all_near, all_opp):
        group.finish()
    for op in sent:
        op.wait_send()


TILES = 2 * NYH + 2
SLOTS = 13 + 12 + 3 * (NX + NZ + NY) + 3 * (NZ + 2 * NX)


def gather_and_gram(snapshot, all_cells):
    cols = snapshot.shape[1]
    vmem = pl.BlockSpec(memory_space=pltpu.VMEM)
    return pl.pallas_call(
        functools.partial(gram_kernel, all_cells),
        out_shape=(jax.ShapeDtypeStruct((G, ROWS, cols), bf16),
                   jax.ShapeDtypeStruct((G, ROWS, cols), bf16),
                   jax.ShapeDtypeStruct((2, NX, NZ, TILES, 8, 128), f32)),
        in_specs=[vmem],
        out_specs=(vmem, vmem, vmem),
        scratch_shapes=[
            pltpu.VMEM((G, ROWS, cols), f32),
            pltpu.VMEM((NX, KINDS, NZ, 8, 128), f32),
            pltpu.VMEM((NX - 1, KINDS, NZ, 8, 128), f32),
            pltpu.VMEM((KINDS, NZ, 8, 128), f32),
            pltpu.VMEM((NZ - 1, KINDS, 8, 128), f32),
            pltpu.VMEM((NY, KINDS, 8, 128), f32),
            pltpu.SemaphoreType.DMA((SLOTS,)),
            pltpu.SemaphoreType.DMA((SLOTS,)),
            pltpu.SemaphoreType.DMA,
        ],
        compiler_params=pltpu.CompilerParams(
            collective_id=0, has_side_effects=True, vmem_limit_bytes=28 * 2**20),
    )(snapshot)


def dot(a, b):
    return lax.dot_general(a, b, (((1,), (0,)), ((), ())), preferred_element_type=f32)


def dot3(a, b_hi, b_lo, nt=False):
    d = dot_nt if nt else dot
    m = a.shape[0]
    a_hi, a_lo = split2(a)
    both = d(jnp.concatenate([a_hi, a_lo], axis=0), b_hi)
    return both[:m] + (both[m:] + d(a_hi, b_lo))


def reciprocal(x):
    r = pl.reciprocal(x, approx=True)
    return r * (2.0 - x * r)


def inverse_factor(m, w_ref):
    n = RANK
    lane = lax.broadcasted_iota(jnp.int32, (8, 128), 1)
    row = lax.broadcasted_iota(jnp.int32, (8, 128), 0)
    js = range(8)
    full = lambda v: jnp.broadcast_to(v, (8, 128))

    def stack(rows):
        t = rows[0]
        for j in js[1:]:
            t = jnp.where(row == j, rows[j], t)
        return t

    rest = jnp.concatenate([m, jnp.zeros((n, 256 - n), f32)], axis=1)
    for p0 in range(0, n, PANEL):
        tiles = [[rest[8 * i:8 * i + 8, 128 * h:128 * h + 128] for h in range(2)] for i in range(PANEL // 8)]
        below = rest[PANEL:]
        ct = p0 // 128
        for gi in range(PANEL // 8):
            c0 = p0 + 8 * gi
            cl = c0 - 128 * ct
            here = (lane >= cl) & (lane < cl + 8)
            t = tiles[gi]
            piv = [[None] * 8 for _ in js]
            for j in js:
                col = full(t[ct][:, cl + j:cl + j + 1])
                for i in range(j + 1):
                    piv[i][j] = full(col[i:i + 1])
            r = [[full(t[h][j:j + 1]) for h in range(2)] for j in js]
            for j in js:
                r[j][ct] = jnp.where(here, jnp.where(lane == cl + j, 1.0, 0.0), r[j][ct])
            inv = [None] * 8
            for j in js:
                inv[j] = reciprocal(piv[j][j])
                for i in range(j + 1, 8):
                    l = piv[j][i] * inv[j]
                    for k in range(i, 8):
                        piv[i][k] = piv[i][k] - l * piv[j][k]
                    for h in range(2):
                        r[i][h] = r[i][h] - l * r[j][h]
            for h in range(2):
                w = stack([r[j][h] * lax.rsqrt(piv[j][j]) for j in js])
                w_ref[c0:c0 + 8, 128 * h:128 * h + 128] = jnp.where(lane + 128 * h <= row + c0, w, 0.0)
            z = [None] * 8
            for j in reversed(js):
                z[j] = []
                for h in range(2):
                    v = r[j][h]
                    for i in range(7, j, -1):
                        v = v - piv[j][i] * z[i][h]
                    z[j].append(v * inv[j])
            for i in range(PANEL // 8):
                if i == gi:
                    continue
                cols = [full(tiles[i][ct][:, cl + j:cl + j + 1]) for j in js]
                old = tiles[i]
                tiles[i] = []
                for h in range(2):
                    v = jnp.where(here, 0.0, old[h]) if h == ct else old[h]
                    even = sum(cols[j] * z[j][h] for j in js[0::2])
                    odd = sum(cols[j] * z[j][h] for j in js[1::2])
                    tiles[i].append(v - (even + odd))
            tiles[gi] = [stack([z[j][h] for j in js]) for h in range(2)]
        if p0 + PANEL < n:
            a = jnp.concatenate([jnp.concatenate(t, axis=1) for t in tiles], axis=0)
            parts = [a]
            if p0 > 128 * ct:
                parts = [jnp.zeros((p0 - 128 * ct, 256), f32)] + parts
            after = 128 * ct + 128 - p0 - PANEL
            if after:
                parts = parts + [jnp.zeros((after, 256), f32)]
            z_hi, z_lo = split2(jnp.concatenate(parts, axis=0))
            lanes = lax.broadcasted_iota(jnp.int32, (1, 256), 1)
            in_panel = (lanes >= p0) & (lanes < p0 + PANEL)
            cut = [below[:PANEL], below[PANEL:]] if below.shape[0] > PANEL else [below]
            rest = jnp.concatenate([
                jnp.where(in_panel, 0.0, v) - dot3(v[:, 128 * ct:128 * ct + 128], z_hi, z_lo) for v in cut], axis=0)


def iterate_kernel(hi_ref, lo_ref, f_ref, start_ref, basis_ref, out_ref, g_hi, g_lo, i_ref, w_ref):
    g = lax.axis_index("gx")


    def store(i, j, block):
        hi, lo = split2(block)
        g_hi[ROWS * i:ROWS * (i + 1), ROWS * j:ROWS * (j + 1)] = hi
        g_lo[ROWS * i:ROWS * (i + 1), ROWS * j:ROWS * (j + 1)] = lo

    def rows(core, tile, first, count):
        own = [f_ref[core, k, :, tile].reshape(NZ * 8, 128)[first:first + count] for k in range(NX)]
        return jnp.concatenate(own, axis=0)

    for yh in range(NYH):
        a, b = 2 * yh, 2 * yh + 1
        pair = jnp.concatenate([rows(0, yh, 32, 16), rows(1, yh, 32, 16)], axis=0)
        store(a, b, pair)
        store(b, a, pair.T)
        for core in range(2):
            i = 2 * yh + core
            store(i, i, rows(core, yh, 0, 32))
            for c in range(2):
                j = 2 * ((yh + 1) % NYH) + c
                block = rows(core, NYH + yh, 32 * c, 32)
                store(i, j, block)
                store(j, i, block.T)
                if yh < 2:
                    j = 2 * (yh + 2) + c
                    block = rows(core, 2 * NYH + yh, 32 * c, 32)
                    store(i, j, block)
                    store(j, i, block.T)

    i_ref[...] = dot3(start_ref[...], g_hi[...], g_lo[...])

    def factor(i_hi, i_lo):
        both = dot_nt(jnp.concatenate([i_hi, i_lo], axis=0), i_hi)
        inverse_factor(both[:RANK] + (both[RANK:] + dot_nt(i_hi, i_lo)), w_ref)

    def times(i_hi, i_lo, b_hi, b_lo):
        both = dot(jnp.concatenate([i_hi, i_lo], axis=0), b_hi)
        return both[:RANK] + (both[RANK:] + dot(i_hi, b_lo))

    def step(_, carry):
        i_hi, i_lo = split2(i_ref[...])
        after = times(i_hi, i_lo, g_hi[...], g_lo[...])
        factor(i_hi, i_lo)
        i_ref[...] = dot3(w_ref[:, :RANK], *split2(after))
        return carry

    lax.fori_loop(0, ITERS - 1, step, 0)
    i_hi, i_lo = split2(i_ref[...])
    after = times(i_hi, i_lo, hi_ref[...], lo_ref[...])
    factor(i_hi, i_lo)
    w = w_ref[:, :RANK]
    core = dot3(w, *split2(after))
    mine_t = dot3(w, *split2(i_ref[:, pl.ds(pl.multiple_of(g * ROWS, ROWS), ROWS)]))
    basis_ref[...] = mine_t
    out_ref[...] = dot3(mine_t.T, *split2(core))


def iterate(d_hi, d_lo, sums, start_t):
    cols = d_hi.shape[1]
    vmem = pl.BlockSpec(memory_space=pltpu.VMEM)
    return pl.pallas_call(
        iterate_kernel,
        out_shape=(jax.ShapeDtypeStruct((RANK, ROWS), f32), jax.ShapeDtypeStruct((ROWS, cols), f32)),
        in_specs=[vmem] * 4,
        out_specs=(vmem, vmem),
        scratch_shapes=[
            pltpu.VMEM((N, N), bf16), pltpu.VMEM((N, N), bf16),
            pltpu.VMEM((RANK, N), f32), pltpu.VMEM((RANK, 256), f32)],
        compiler_params=pltpu.CompilerParams(vmem_limit_bytes=28 * 2**20),
    )(d_hi, d_lo, sums, start_t)


def body(snapshot, start):
    all_cells = snapshot.shape[1] * lax.axis_size("yz")
    d_hi, d_lo, sums = gather_and_gram(snapshot, all_cells)
    shape = (N, snapshot.shape[1])
    basis_t, projected = iterate(d_hi.reshape(shape), d_lo.reshape(shape), sums, start.T)
    return basis_t.T, projected


def solution(mesh):
    in_specs = (P("gx", "yz"), P())
    out_specs = (P("gx", None), P("gx", "yz"))
    return jax.shard_map(body, mesh=mesh, in_specs=in_specs, out_specs=out_specs, check_vma=False)
```

```python
import functools
import jax
import jax.numpy as jnp
from jax import lax
from jax.experimental import pallas as pl
from jax.experimental.pallas import tpu as pltpu
from jax.sharding import PartitionSpec as P

ITERS = 4
G, NYH, NZ, NX, NYL, NY = 8, 4, 8, 4, 2, 8
ROWS = 128
KINDS = 4
RING_ORDER = (4, 3, 5, 2, 6, 1, 7)
N = 1024
RANK = 192
PANEL = 32
f32, bf16 = jnp.float32, jnp.bfloat16
MESH = pl.DeviceIdType.MESH


def split2(a):
    hi = a.astype(jnp.bfloat16)
    lo = (a - hi.astype(jnp.float32)).astype(jnp.bfloat16)
    return hi, lo


def dot_nt(a, b):
    return lax.dot_general(a, b, (((1,), (1,)), ((), ())), preferred_element_type=jnp.float32)


def gram_kernel(cells, s_ref, hi_ref, lo_ref, f_ref, d_ref, parts, xin, xsum, zin, ysum, send, recv, local):
    g = lax.axis_index("gx")
    q = lax.axis_index("yz")
    yh, core = g // 2, g % 2
    z, x, yl = q // (NX * NYL), (q // NYL) % NX, q % NYL
    y = yh * NYL + yl

    def gx_at(yh2, core2):
        return (yh2 % NYH) * 2 + core2

    def yz_at(z2, x2, yl2):
        return ((z2 % NZ) * NX + x2 % NX) * NYL + yl2

    def y_peer(y2):
        return (gx_at((y2 % NY) // NYL, core), yz_at(z, x, y2 % NYL))

    def x_peer(k):
        return (g, yz_at(z, x + k, yl))

    def z_peer(k):
        return (g, yz_at(z + k, x, yl))

    pair = (gx_at(yh, 1 - core), q)
    right, left = (gx_at(yh + 1, core), q), (gx_at(yh + 3, core), q)
    peers = [pair] + [y_peer(y + k) for k in range(1, NY)]
    peers += [x_peer(k) for k in range(1, NX)] + [z_peer(k) for k in range(1, NZ)]

    barrier = pltpu.get_barrier_semaphore()
    for peer in peers:
        pl.semaphore_signal(barrier, inc=1, device_id=peer, device_id_type=MESH)
    mine = pltpu.make_async_copy(s_ref, d_ref.at[g], local)
    mine.start()
    pl.semaphore_wait(barrier, len(peers))

    sent = []
    count = [0]

    def slot(n=1):
        count[0] += n
        return count[0] - n

    def copy(src, dst, index, target):
        return pltpu.make_async_remote_copy(
            src_ref=src, dst_ref=dst, send_sem=send.at[index], recv_sem=recv.at[index],
            device_id=target, device_id_type=MESH)

    def push(ref, index, target, src=None):
        op = copy(ref if src is None else src, ref, index, target)
        op.start()
        sent.append(op)

    def arrived(ref, index):
        copy(ref, ref, index, pair).wait_recv()

    quarter = s_ref.shape[1] // 4
    mine_q = yh // 2
    far_q = 1 - mine_q
    right_q = 1 - (yh + 1) % NYH // 2
    left_q = 1 - (yh + 3) % NYH // 2

    def lanes(first, n):
        return pl.ds(pl.multiple_of(first * quarter, quarter), n * quarter)

    def cells_of(block, first, n=1):
        return d_ref.at[block, :, lanes(first, n)]

    def own(first, n=1):
        return s_ref.at[:, lanes(first, n)]

    g_right, g_left, g_opp = right[0], left[0], gx_at(yh + 2, core)
    p_own = pair[0]
    p_right, p_left, p_opp = (gx_at(yh + k, 1 - core) for k in (1, 3, 2))
    s_pair, s_down, s_up, s_relay = slot(), slot(2), slot(2), slot(2)
    f_right, f_left, f_opp = slot(2), slot(2), slot(2)
    push(cells_of(g, far_q), s_down, left, own(far_q))
    push(cells_of(g, 2 + far_q), s_up, right, own(2 + far_q))
    push(d_ref.at[g], s_pair, pair, s_ref)
    push(cells_of(g, mine_q), s_down + 1, left, own(mine_q))
    push(cells_of(g, 2 + mine_q), s_up + 1, right, own(2 + mine_q))

    def split_into(block, first, n):
        where = lanes(first, n)
        hi_ref[block, :, where], lo_ref[block, :, where] = split2(d_ref[block, :, where])

    def product(a, b, segments, first=0, rows=ROWS):
        total = None
        for begin, n in segments:
            where = lanes(begin, n)
            a_hi, a_lo = hi_ref[a, pl.ds(first, rows), where], lo_ref[a, pl.ds(first, rows), where]
            b_hi, b_lo = hi_ref[b, :, where], lo_ref[b, :, where]
            both = dot_nt(jnp.concatenate([a_hi, a_lo], axis=0), b_hi)
            term = both[:rows] + (both[rows:] + dot_nt(a_hi, b_lo))
            total = term if total is None else total + term
        return total * (1.0 / cells)

    def put(kind, position, block):
        rows = block.shape[0] // NX
        for k in range(NX):
            parts[k, kind, pl.ds(position, rows // 8)] = block[rows * k:rows * (k + 1)].reshape(rows // 8, 8, 128)

    class Sums:
        def __init__(self, lo, n):
            self.kinds = pl.ds(lo, n)
            self.x, self.z, self.y = slot(NX), slot(NZ), slot(NY)

        def send_x(self):
            for k in (2, 1, 3):
                push(xin.at[k - 1, self.kinds], self.x + k, x_peer(k), parts.at[(x + k) % NX, self.kinds])

        def send_z(self):
            total = parts[x, self.kinds]
            for k in range(1, NX):
                arrived(xin.at[k - 1, self.kinds], self.x + k)
                total += xin[k - 1, self.kinds]
            xsum[self.kinds] = total
            for k in RING_ORDER:
                push(zin.at[k - 1, self.kinds], self.z + k, z_peer(k), xsum.at[self.kinds, (z + k) % NZ])

        def send_y(self):
            total = xsum[self.kinds, z]
            for k in range(1, NZ):
                arrived(zin.at[k - 1, self.kinds], self.z + k)
                total += zin[k - 1, self.kinds]
            ysum[y, self.kinds] = total
            for k in RING_ORDER:
                push(ysum.at[y, self.kinds], self.y + k, y_peer(y + k))

        def finish(self):
            for k in range(1, NY):
                arrived(ysum.at[(y + NY - k) % NY, self.kinds], self.y + k)

    class Spread:
        def __init__(self, lo, n):
            self.tiles = pl.ds(lo, n)
            self.z, self.x, self.pair = slot(NZ), slot(NX), slot(NX)

        def part(self, core2, k):
            return f_ref.at[core2, (x + NX - k) % NX, :, self.tiles]

        def send_z(self):
            for k in RING_ORDER:
                push(f_ref.at[core, x, z, self.tiles], self.z + k, z_peer(k))

        def send_x(self):
            for k in range(1, NZ):
                arrived(f_ref.at[core, x, (z + NZ - k) % NZ, self.tiles], self.z + k)
            for k in (2, 1, 3):
                push(self.part(core, 0), self.x + k, x_peer(k))
            push(self.part(core, 0), self.pair, pair)

        def send_pair(self):
            for k in (1, 3, 2):
                arrived(self.part(core, k), self.x + k)
                push(self.part(core, k), self.pair + k, pair)

        def finish(self):
            for k in range(NX):
                arrived(self.part(1 - core, k), self.pair + k)

    sum_own, sum_near, sum_opp = Sums(0, 1), Sums(1, 2), Sums(3, 1)
    all_own, all_near, all_opp = Spread(0, NYH), Spread(NYH, NYH), Spread(2 * NYH, 2)

    mine.wait()
    split_into(g, 0, 4)
    put(0, 0, product(g, g, [(0, 4)]))
    arrived(d_ref.at[p_own], s_pair)
    split_into(p_own, 0, 4)
    halfrows = ROWS // 2
    first = pl.multiple_of(halfrows * core, halfrows)
    put(0, 4, product(gx_at(yh, 0), gx_at(yh, 1), [(0, 4)], first, halfrows))
    for k in range(NX):
        parts[k, 0, 6:8] = jnp.zeros((2, 8, 128), f32)
    sum_own.send_x()

    arrived(cells_of(g_right, right_q), s_down)
    push(cells_of(g_right, right_q), s_relay, left)
    push(cells_of(g_right, right_q), f_right, pair)
    arrived(cells_of(g_left, 2 + left_q), s_up)
    push(cells_of(g_left, 2 + left_q), s_relay + 1, right)
    push(cells_of(g_left, 2 + left_q), f_left, pair)
    sum_own.send_z()
    arrived(cells_of(g_right, 1 - right_q), s_down + 1)
    push(cells_of(g_right, 1 - right_q), f_right + 1, pair)
    arrived(cells_of(g_left, 3 - left_q), s_up + 1)
    push(cells_of(g_left, 3 - left_q), f_left + 1, pair)
    sum_own.send_y()
    split_into(g_right, 0, 2)
    split_into(g_left, 2, 2)
    for c in range(2):
        put(2, 4 * c, product(g_left, gx_at(yh, c), [(2, 2)]))
    put(1, 4 * core, product(g, g_right, [(0, 2)]))
    arrived(cells_of(p_right, right_q), f_right)
    arrived(cells_of(p_right, 1 - right_q), f_right + 1)
    split_into(p_right, 0, 2)
    put(1, 4 * (1 - core), product(g, p_right, [(0, 2)]))
    sum_near.send_x()
    l_right, l_left, l_relay, l_pair = slot(2), slot(2), slot(2), slot(6)
    push(cells_of(g_right, 1 - right_q), l_relay, left)
    push(cells_of(g_left, 3 - left_q), l_relay + 1, right)
    sum_own.finish()
    for k in range(NYH):
        f_ref[core, x, z, k] = ysum[2 * k, 0] + ysum[2 * k + 1, 0]
    all_own.send_z()

    arrived(cells_of(g_opp, mine_q), s_relay)
    push(cells_of(g_opp, mine_q), f_opp, pair)
    arrived(cells_of(g_opp, 2 + mine_q), s_relay + 1)
    push(cells_of(g_opp, 2 + mine_q), f_opp + 1, pair)
    push(cells_of(g, 0), l_right, right, own(0))
    push(cells_of(g, 2), l_left, left, own(2))
    split_into(g_opp, mine_q, 1)
    split_into(g_opp, 2 + mine_q, 1)
    sum_near.send_z()
    segments = [(mine_q, 1), (2 + mine_q, 1)]
    put(3, 4 * core, product(gx_at(yh % 2, core), gx_at(yh % 2 + 2, core), segments))
    arrived(cells_of(p_opp, mine_q), f_opp)
    split_into(p_opp, mine_q, 1)
    arrived(cells_of(p_opp, 2 + mine_q), f_opp + 1)
    split_into(p_opp, 2 + mine_q, 1)
    put(3, 4 * (1 - core), product(gx_at(yh % 2, core), gx_at(yh % 2 + 2, 1 - core), segments))
    sum_opp.send_x()
    all_own.send_x()
    sum_near.send_y()
    sum_opp.send_z()
    sum_near.finish()
    for k in range(NYH):
        after = (k + 1) % NYH
        f_ref[core, x, z, NYH + k] = (ysum[2 * k, 1] + ysum[2 * k + 1, 1]) + (ysum[2 * after, 2] + ysum[2 * after + 1, 2])
    all_near.send_z()
    sum_opp.send_y()
    push(cells_of(g, 1), l_right + 1, right, own(1))
    push(cells_of(g, 3), l_left + 1, left, own(3))
    all_own.send_pair()
    sum_opp.finish()
    for k in range(2):
        f_ref[core, x, z, 2 * NYH + k] = (ysum[2 * k, 3] + ysum[2 * k + 1, 3]) + (ysum[2 * k + 4, 3] + ysum[2 * k + 5, 3])
    all_opp.send_z()
    all_near.send_x()
    for k in range(2):
        arrived(cells_of(g_opp, 2 * k + far_q), l_relay + k)
        push(cells_of(g_opp, 2 * k + far_q), l_pair + k, pair)
    arrived(cells_of(g_left, 0), l_right)
    push(cells_of(g_left, 0), l_pair + 2, pair)
    arrived(cells_of(g_right, 2), l_left)
    push(cells_of(g_right, 2), l_pair + 3, pair)
    split_into(g_opp, far_q, 1)
    split_into(g_opp, 2 + far_q, 1)
    all_opp.send_x()
    arrived(cells_of(p_left, 2 + left_q), f_left)
    arrived(cells_of(p_left, 3 - left_q), f_left + 1)
    split_into(p_left, 2, 2)
    all_near.send_pair()
    for k in range(2):
        arrived(cells_of(p_opp, 2 * k + far_q), l_pair + k)
        split_into(p_opp, 2 * k + far_q, 1)
    all_opp.send_pair()
    arrived(cells_of(g_left, 1), l_right + 1)
    push(cells_of(g_left, 1), l_pair + 4, pair)
    arrived(cells_of(g_right, 3), l_left + 1)
    push(cells_of(g_right, 3), l_pair + 5, pair)
    split_into(g_left, 0, 2)
    split_into(g_right, 2, 2)
    arrived(cells_of(p_left, 0), l_pair + 2)
    arrived(cells_of(p_left, 1), l_pair + 4)
    split_into(p_left, 0, 2)
    arrived(cells_of(p_right, 2), l_pair + 3)
    arrived(cells_of(p_right, 3), l_pair + 5)
    split_into(p_right, 2, 2)
    for group in (all_own, all_near, all_opp):
        group.finish()
    for op in sent:
        op.wait_send()


TILES = 2 * NYH + 2
SLOTS = 13 + 12 + 3 * (NX + NZ + NY) + 3 * (NZ + 2 * NX)


def gather_and_gram(snapshot, all_cells):
    cols = snapshot.shape[1]
    vmem = pl.BlockSpec(memory_space=pltpu.VMEM)
    return pl.pallas_call(
        functools.partial(gram_kernel, all_cells),
        out_shape=(jax.ShapeDtypeStruct((G, ROWS, cols), bf16),
                   jax.ShapeDtypeStruct((G, ROWS, cols), bf16),
                   jax.ShapeDtypeStruct((2, NX, NZ, TILES, 8, 128), f32)),
        in_specs=[vmem],
        out_specs=(vmem, vmem, vmem),
        scratch_shapes=[
            pltpu.VMEM((G, ROWS, cols), f32),
            pltpu.VMEM((NX, KINDS, NZ, 8, 128), f32),
            pltpu.VMEM((NX - 1, KINDS, NZ, 8, 128), f32),
            pltpu.VMEM((KINDS, NZ, 8, 128), f32),
            pltpu.VMEM((NZ - 1, KINDS, 8, 128), f32),
            pltpu.VMEM((NY, KINDS, 8, 128), f32),
            pltpu.SemaphoreType.DMA((SLOTS,)),
            pltpu.SemaphoreType.DMA((SLOTS,)),
            pltpu.SemaphoreType.DMA,
        ],
        compiler_params=pltpu.CompilerParams(
            collective_id=0, has_side_effects=True, vmem_limit_bytes=28 * 2**20),
    )(snapshot)


def dot(a, b):
    return lax.dot_general(a, b, (((1,), (0,)), ((), ())), preferred_element_type=f32)


def dot3(a, b_hi, b_lo, nt=False):
    d = dot_nt if nt else dot
    m = a.shape[0]
    a_hi, a_lo = split2(a)
    both = d(jnp.concatenate([a_hi, a_lo], axis=0), b_hi)
    return both[:m] + (both[m:] + d(a_hi, b_lo))


def reciprocal(x):
    return pl.reciprocal(x, approx=True)


def inverse_factor(m, w_ref):
    n = RANK
    lane = lax.broadcasted_iota(jnp.int32, (8, 128), 1)
    row = lax.broadcasted_iota(jnp.int32, (8, 128), 0)
    js = range(8)
    full = lambda v: jnp.broadcast_to(v, (8, 128))

    def stack(rows):
        t = rows[0]
        for j in js[1:]:
            t = jnp.where(row == j, rows[j], t)
        return t

    rest = jnp.concatenate([m, jnp.zeros((n, 256 - n), f32)], axis=1)
    for p0 in range(0, n, PANEL):
        tiles = [[rest[8 * i:8 * i + 8, 128 * h:128 * h + 128] for h in range(2)] for i in range(PANEL // 8)]
        below = rest[PANEL:]
        ct = p0 // 128
        for gi in range(PANEL // 8):
            c0 = p0 + 8 * gi
            cl = c0 - 128 * ct
            here = (lane >= cl) & (lane < cl + 8)
            t = tiles[gi]
            piv = [[None] * 8 for _ in js]
            for j in js:
                col = full(t[ct][:, cl + j:cl + j + 1])
                for i in range(j + 1):
                    piv[i][j] = full(col[i:i + 1])
            r = [[full(t[h][j:j + 1]) for h in range(2)] for j in js]
            for j in js:
                r[j][ct] = jnp.where(here, jnp.where(lane == cl + j, 1.0, 0.0), r[j][ct])
            inv = [None] * 8
            for j in js:
                inv[j] = reciprocal(piv[j][j])
                for i in range(j + 1, 8):
                    l = piv[j][i] * inv[j]
                    for k in range(i, 8):
                        piv[i][k] = piv[i][k] - l * piv[j][k]
                    for h in range(2):
                        r[i][h] = r[i][h] - l * r[j][h]
            for h in range(2):
                w = stack([r[j][h] * lax.rsqrt(piv[j][j]) for j in js])
                w_ref[c0:c0 + 8, 128 * h:128 * h + 128] = jnp.where(lane + 128 * h <= row + c0, w, 0.0)
            z = [None] * 8
            for j in reversed(js):
                z[j] = []
                for h in range(2):
                    v = r[j][h]
                    for i in range(7, j, -1):
                        v = v - piv[j][i] * z[i][h]
                    z[j].append(v * inv[j])
            for i in range(PANEL // 8):
                if i == gi:
                    continue
                cols = [full(tiles[i][ct][:, cl + j:cl + j + 1]) for j in js]
                old = tiles[i]
                tiles[i] = []
                for h in range(2):
                    v = jnp.where(here, 0.0, old[h]) if h == ct else old[h]
                    even = sum(cols[j] * z[j][h] for j in js[0::2])
                    odd = sum(cols[j] * z[j][h] for j in js[1::2])
                    tiles[i].append(v - (even + odd))
            tiles[gi] = [stack([z[j][h] for j in js]) for h in range(2)]
        if p0 + PANEL < n:
            a = jnp.concatenate([jnp.concatenate(t, axis=1) for t in tiles], axis=0)
            parts = [a]
            if p0 > 128 * ct:
                parts = [jnp.zeros((p0 - 128 * ct, 256), f32)] + parts
            after = 128 * ct + 128 - p0 - PANEL
            if after:
                parts = parts + [jnp.zeros((after, 256), f32)]
            z_hi, z_lo = split2(jnp.concatenate(parts, axis=0))
            lanes = lax.broadcasted_iota(jnp.int32, (1, 256), 1)
            in_panel = (lanes >= p0) & (lanes < p0 + PANEL)
            cut = [below[:PANEL], below[PANEL:]] if below.shape[0] > PANEL else [below]
            rest = jnp.concatenate([
                jnp.where(in_panel, 0.0, v) - dot3(v[:, 128 * ct:128 * ct + 128], z_hi, z_lo) for v in cut], axis=0)


def iterate_kernel(hi_ref, lo_ref, f_ref, start_ref, basis_ref, out_ref, g_hi, g_lo, i_ref, w_ref):
    g = lax.axis_index("gx")


    def store(i, j, block):
        hi, lo = split2(block)
        g_hi[ROWS * i:ROWS * (i + 1), ROWS * j:ROWS * (j + 1)] = hi
        g_lo[ROWS * i:ROWS * (i + 1), ROWS * j:ROWS * (j + 1)] = lo

    def rows(core, tile, first, count):
        own = [f_ref[core, k, :, tile].reshape(NZ * 8, 128)[first:first + count] for k in range(NX)]
        return jnp.concatenate(own, axis=0)

    for yh in range(NYH):
        a, b = 2 * yh, 2 * yh + 1
        pair = jnp.concatenate([rows(0, yh, 32, 16), rows(1, yh, 32, 16)], axis=0)
        store(a, b, pair)
        store(b, a, pair.T)
        for core in range(2):
            i = 2 * yh + core
            store(i, i, rows(core, yh, 0, 32))
            for c in range(2):
                j = 2 * ((yh + 1) % NYH) + c
                block = rows(core, NYH + yh, 32 * c, 32)
                store(i, j, block)
                store(j, i, block.T)
                if yh < 2:
                    j = 2 * (yh + 2) + c
                    block = rows(core, 2 * NYH + yh, 32 * c, 32)
                    store(i, j, block)
                    store(j, i, block.T)

    i_ref[...] = dot3(start_ref[...], g_hi[...], g_lo[...])

    def factor(i_hi, i_lo):
        both = dot_nt(jnp.concatenate([i_hi, i_lo], axis=0), i_hi)
        inverse_factor(both[:RANK] + (both[RANK:] + dot_nt(i_hi, i_lo)), w_ref)

    def times(i_hi, i_lo, b_hi, b_lo):
        both = dot(jnp.concatenate([i_hi, i_lo], axis=0), b_hi)
        return both[:RANK] + (both[RANK:] + dot(i_hi, b_lo))

    def step(_, carry):
        i_hi, i_lo = split2(i_ref[...])
        after = times(i_hi, i_lo, g_hi[...], g_lo[...])
        factor(i_hi, i_lo)
        i_ref[...] = dot3(w_ref[:, :RANK], *split2(after))
        return carry

    lax.fori_loop(0, ITERS - 1, step, 0)
    i_hi, i_lo = split2(i_ref[...])
    after = times(i_hi, i_lo, hi_ref[...], lo_ref[...])
    factor(i_hi, i_lo)
    w = w_ref[:, :RANK]
    core = dot3(w, *split2(after))
    mine_t = dot3(w, *split2(i_ref[:, pl.ds(pl.multiple_of(g * ROWS, ROWS), ROWS)]))
    basis_ref[...] = mine_t
    out_ref[...] = dot3(mine_t.T, *split2(core))


def iterate(d_hi, d_lo, sums, start_t):
    cols = d_hi.shape[1]
    vmem = pl.BlockSpec(memory_space=pltpu.VMEM)
    return pl.pallas_call(
        iterate_kernel,
        out_shape=(jax.ShapeDtypeStruct((RANK, ROWS), f32), jax.ShapeDtypeStruct((ROWS, cols), f32)),
        in_specs=[vmem] * 4,
        out_specs=(vmem, vmem),
        scratch_shapes=[
            pltpu.VMEM((N, N), bf16), pltpu.VMEM((N, N), bf16),
            pltpu.VMEM((RANK, N), f32), pltpu.VMEM((RANK, 256), f32)],
        compiler_params=pltpu.CompilerParams(vmem_limit_bytes=28 * 2**20),
    )(d_hi, d_lo, sums, start_t)


def body(snapshot, start):
    all_cells = snapshot.shape[1] * lax.axis_size("yz")
    d_hi, d_lo, sums = gather_and_gram(snapshot, all_cells)
    shape = (N, snapshot.shape[1])
    basis_t, projected = iterate(d_hi.reshape(shape), d_lo.reshape(shape), sums, start.T)
    return basis_t.T, projected


def solution(mesh):
    in_specs = (P("gx", "yz"), P())
    out_specs = (P("gx", None), P("gx", "yz"))
    return jax.shard_map(body, mesh=mesh, in_specs=in_specs, out_specs=out_specs, check_vma=False)
```
